128 devices in a mesh: grp: 2 (over y_hi), dev: 64 (over z, x, y_lo, core).
Axes of the slice: x: 4, y: 4 (y_hi: 2, y_lo: 2; y = y_hi * 2 + y_lo), z: 4, core: 2. Of those that a mesh axis runs over, the one named last changes fastest.
Arguments:
- hidden: bfloat16 [512, 7168], P(('grp', 'dev')), may hold values from -6 to 6
- queries: bfloat16 [512, 16384], P(('grp', 'dev')), may hold values from -120 to 120
- new_key: bfloat16 [512, 256], P(('grp', 'dev')), may hold values from -6 to 6
- new_value: bfloat16 [512, 256], P(('grp', 'dev')), may hold values from -6 to 6
- cache_keys: bfloat16 [512, 2048, 256], P(('grp', 'dev')), may hold values from -6 to 6
- cache_values: bfloat16 [512, 2048, 256], P(('grp', 'dev')), may hold values from -6 to 6
- lengths: int32 [512], P(('grp', 'dev')), may hold values from 2 to 2048, as said below
- out_weight: bfloat16 [16384, 7168], P(None, 'dev'), may hold values from -0.375 to 0.375
- ffn_gain: float32 [7168], replicated, may hold values from 0.5 to 1.5
- gate_weight: bfloat16 [7168, 40960], P(None, ('grp', 'dev')), may hold values from -0.0625 to 0.0625
- up_weight: bfloat16 [7168, 40960], P(None, ('grp', 'dev')), may hold values from -0.0625 to 0.0625
- down_weight: bfloat16 [40960, 7168], P(('grp', 'dev')), may hold values from -0.078125 to 0.078125
- routes: int32 [512, 3], P(('grp', 'dev')), may hold values from 0 to 7, as said below
- route_gates: int32 [512, 3], P(('grp', 'dev')), may hold values from 1 to 255
Outputs:
- layer_out: bfloat16 [512, 7168], P(('grp', 'dev'))
The draws below stay inside these ranges and needn't reach their ends.
Inputs may be any that keep to these rules, and one draw needn't show every extreme that they name: `lengths`: some row has all 2048 positions filled. `routes`: each row names 3 different experts; among the rows of one device no expert is named by more than 2 rows, and one expert, the same for all devices and drawn afresh, is named by exactly 2 rows of every device.
All inputs are finite; a program needn't handle non-finite values.
Results may differ from the reference program's by a relative error of at most 0.0095.
Values may be sent and summed in bfloat16 or wider, within the bound.
No kernel may reach another device: no remote copies, remote signals or barrier semaphores. Data moves between devices by JAX's collectives and lax.ppermute only.
A program may use at most 128 MiB of HBM per device.

```python
import math
import jax
import jax.numpy as jnp
from jax import lax

D = 7168
HEADS = 64
HEAD = 256
HID = 5120
TOP = 3
EXPERTS = 8
ROWS_DEV = 4
CTX = 2048
ROWS = 512


def leading_keys(key):
    return jnp.clip(jax.random.normal(jax.random.fold_in(key, 101), (ROWS, HEAD), jnp.float32), -6.0, 6.0)


def draw_cache_keys(key, part):
    leading = leading_keys(key)
    key = jax.random.fold_in(key, 5)
    remaining = jnp.clip(jax.random.normal(key, (ROWS, CTX - 1, HEAD), jnp.float32), -6.0, 6.0)
    joined = jnp.concatenate([leading[:, None, :], remaining], axis=1)
    return joined.astype(jnp.bfloat16)


def draw_queries(key, part):
    key = jax.random.fold_in(key, 7)
    queried = 1.5 * jnp.clip(jax.random.normal(key, (ROWS, HEADS, HEAD), jnp.float32), -4.0, 4.0)
    return queried.reshape(ROWS, HEADS * HEAD).astype(jnp.bfloat16)


def draw_lengths(key, part):
    key = jax.random.fold_in(key, 9)
    filled = jax.random.randint(key, (ROWS,), 2, CTX + 1, dtype=jnp.int32)
    return filled.at[0].set(CTX)


def draw_routes(key, part):
    key = jax.random.fold_in(key, 13)
    block = ROWS_DEV
    capacity = ROWS_DEV // 2
    blocks = ROWS // ROWS_DEV
    popular_key, blocks_key = jax.random.split(key, 2)
    popular = jax.random.randint(popular_key, (), 0, EXPERTS, dtype=jnp.int32)
    tail = EXPERTS * capacity - capacity

    def one_block(block_key):
        order_key, drop_key, shuffle_key, turn_key = jax.random.split(block_key, 4)
        others = jax.random.permutation(order_key, EXPERTS - 1).astype(jnp.int32)
        others = others + (others >= popular).astype(jnp.int32)
        runs = jnp.concatenate([jnp.full((1,), popular, jnp.int32), others])
        sequence = jnp.repeat(runs, capacity, total_repeat_length=EXPERTS * capacity)
        order = jax.random.permutation(drop_key, tail).astype(jnp.int32)
        dropped = (order < block).astype(jnp.int32)
        flags = jnp.concatenate([jnp.zeros((capacity,), jnp.int32), dropped])
        kept = jnp.argsort(flags, stable=True)[:TOP * block]
        picks = sequence[kept]
        table = picks.reshape(TOP, block).T
        shuffle = jax.random.permutation(shuffle_key, block)
        table = table[shuffle]
        turn = jax.random.randint(turn_key, (block,), 0, TOP, dtype=jnp.int32)
        columns = (jnp.arange(TOP, dtype=jnp.int32)[None, :] + turn[:, None]) % TOP
        return jnp.take_along_axis(table, columns, axis=1)
    tables = jax.vmap(one_block)(jax.random.split(blocks_key, blocks))
    return tables.reshape(ROWS, TOP).astype(jnp.int32)


def set_ends(result, stream_key, least, high):
    dims = result.shape
    spot = [jax.random.randint(jax.random.fold_in(stream_key, axis), (), 0, dims[axis]) for axis in range(len(dims))]
    result = result.at[tuple(spot)].set(least)
    longest = dims.index(max(dims))
    spot[longest] = (spot[longest] + 1) % dims[longest]
    return result.at[tuple(spot)].set(high)


def level_of(rng, extent, cuts, least, high):
    loudness = 1.0
    for axis_at, shards_of in cuts:
        heights = jax.random.uniform(jax.random.fold_in(jax.random.fold_in(rng, 6), axis_at), (shards_of,), jnp.float32, least / len(cuts), high / len(cuts))
        loudness = loudness * jnp.repeat(jnp.exp(heights), extent[axis_at] // shards_of).reshape((-1,) + (1,) * (len(extent) - 1 - axis_at))
    return loudness


def noise(stream_key, shape, scale, reach, pieces=(), kind=jnp.bfloat16):
    level = level_of(stream_key, shape, pieces, -0.22, 0.18) if pieces else 1.0
    entries = jax.random.normal(stream_key, shape, jnp.float32) * scale * level
    return jnp.minimum(jnp.maximum(entries, -reach), reach).astype(kind)


def setup_inputs(seed: int = 0) -> dict:
    arg_keys = jax.random.split(jax.random.key(seed), 15)
    hidden = noise(arg_keys[0], (ROWS, D), 1.0, 6.0, ((0, 128),))
    queries = draw_queries(jax.random.fold_in(arg_keys[14], 71), 0)
    new_key = noise(arg_keys[2], (ROWS, HEAD), 1.0, 6.0, ((0, 128),))
    new_value = noise(arg_keys[3], (ROWS, HEAD), 1.0, 6.0, ((0, 128),))
    cache_keys = draw_cache_keys(jax.random.fold_in(arg_keys[14], 71), 0)
    cache_values = noise(arg_keys[5], (ROWS, CTX, HEAD), 1.0, 6.0, ((0, 128),))
    lengths = draw_lengths(jax.random.fold_in(arg_keys[14], 71), 0)
    out_weight = noise(arg_keys[7], (HEADS * HEAD, D), HEAD ** -0.5, 0.375, ((1, 64),))
    ffn_gain = jnp.clip(1.0 + 0.1 * jax.random.normal(arg_keys[8], (D,), jnp.float32), 0.5, 1.5)
    gate_weight = noise(arg_keys[9], (D, EXPERTS * HID), D ** -0.5, 0.0625, ((1, 128),))
    up_weight = noise(arg_keys[10], (D, EXPERTS * HID), D ** -0.5, 0.0625, ((1, 128),))
    down_weight = noise(arg_keys[11], (EXPERTS * HID, D), HID ** -0.5, 0.078125, ((0, 128),))
    routes = draw_routes(jax.random.fold_in(arg_keys[14], 71), 0)
    route_gates = set_ends(jax.random.randint(arg_keys[13], (ROWS, TOP), 1, 256), jax.random.fold_in(arg_keys[13], 1), 1, 255).astype(jnp.int32)
    return dict(hidden=hidden, queries=queries, new_key=new_key, new_value=new_value, cache_keys=cache_keys, cache_values=cache_values, lengths=lengths, out_weight=out_weight, ffn_gain=ffn_gain, gate_weight=gate_weight, up_weight=up_weight, down_weight=down_weight, routes=routes, route_gates=route_gates)


def attend_row(item):
    query_row, keys, values, fresh_key, fresh_value, length = item
    queried = query_row.reshape(HEADS, HEAD)
    scaling = 1.0 / math.sqrt(HEAD)
    cached = jnp.dot(queried, keys.T, preferred_element_type=jnp.float32) * scaling
    itself = jnp.dot(queried, fresh_key, preferred_element_type=jnp.float32) * scaling
    position = jnp.arange(CTX, dtype=jnp.int32)
    cached = jnp.where(position[None, :] < length, cached, -jnp.inf)
    highest = jnp.maximum(lax.optimization_barrier(jnp.max(cached, axis=1)), itself)
    cached_exp = jnp.exp(cached - highest[:, None])
    itself_exp = jnp.exp(itself - highest)
    totals = lax.optimization_barrier(jnp.sum(cached_exp, axis=1)) + itself_exp
    cached_probs = (cached_exp / totals[:, None]).astype(jnp.bfloat16)
    itself_probs = (itself_exp / totals).astype(jnp.bfloat16)
    mixture = jnp.dot(cached_probs, values, preferred_element_type=jnp.float32)
    mixture = mixture + itself_probs.astype(jnp.float32)[:, None] * fresh_value.astype(jnp.float32)[None, :]
    return mixture.astype(jnp.bfloat16).reshape(HEADS * HEAD)

def reference(hidden, queries, new_key, new_value, cache_keys, cache_values, lengths, out_weight, ffn_gain, gate_weight, up_weight, down_weight, routes, route_gates):
    attended = lax.map(attend_row, (queries, cache_keys, cache_values, new_key, new_value, lengths))
    projected = jnp.dot(attended, out_weight, preferred_element_type=jnp.float32)
    mixed = (hidden.astype(jnp.float32) + projected).astype(jnp.bfloat16)
    widened = lax.optimization_barrier(mixed).astype(jnp.float32)
    mean_square = lax.optimization_barrier(jnp.mean(widened * widened, axis=-1, keepdims=True))
    normed = (widened * lax.rsqrt(mean_square + 1e-05) * ffn_gain).astype(jnp.bfloat16)
    weights_int = route_gates.astype(jnp.float32)
    shares = weights_int / lax.optimization_barrier(jnp.sum(weights_int, axis=-1, keepdims=True))
    moe_out = jnp.zeros((ROWS, D), jnp.float32)
    for expert in range(EXPERTS):
        lower = expert * HID
        gated = jnp.dot(normed, gate_weight[:, lower:lower + HID], preferred_element_type=jnp.float32)
        upward = jnp.dot(normed, up_weight[:, lower:lower + HID], preferred_element_type=jnp.float32)
        activated = (jax.nn.silu(gated) * upward).astype(jnp.bfloat16)
        expert_out = jnp.dot(activated, down_weight[lower:lower + HID, :], preferred_element_type=jnp.float32)
        chosen = lax.optimization_barrier(jnp.sum(jnp.where(routes == expert, shares, 0.0), axis=-1))
        moe_out = moe_out + chosen[:, None] * expert_out
    return (widened + moe_out).astype(jnp.bfloat16)
```

```python
import math

import jax
import jax.numpy as jnp
from jax import lax
from jax.experimental import pallas as pl
from jax.experimental.pallas import tpu as pltpu
from jax.sharding import Mesh, PartitionSpec as P

D = 7168
HEAD = 256
KALL = 16384
KHALF = KALL // 2
KQ = KHALF // 2
KE = KQ // 2
HID_DEV = 320
COLS = 112
EXPERTS = 8
BF = jnp.bfloat16
F32 = jnp.float32
SIZES = {"g": 2, "z": 4, "x": 4, "y": 2, "c": 2}
ALL = ("g", "z", "x", "y", "c")
SECTION = ("z", "x", "y", "c")


def shift(array, axis, step=1):
    n = SIZES[axis]
    return lax.ppermute(array, axis, [(i, (i + step) % n) for i in range(n)])


def others4(array, axis):
    return [shift(array, axis, 1), shift(array, axis, 2), shift(array, axis, 3)]


def ring_gy(array, step):
    return lax.ppermute(array, ("g", "y"), [(i, (i + step) % 4) for i in range(4)])


def pair_ordered(own, other, mine):
    return jnp.where(
        mine == 0, jnp.stack([own, other]), jnp.stack([other, own])
    )


def attend(queries, new_key, new_value, cache_keys, cache_values, lengths):
    row_count = queries.shape[0]
    head_size = new_key.shape[1]
    head_count = queries.shape[1] // head_size
    context = cache_keys.shape[1]
    queried = queries.reshape(row_count, head_count, head_size)
    scaling = 1.0 / math.sqrt(head_size)
    cached = (
        jnp.einsum("rhd,rpd->rhp", queried, cache_keys, preferred_element_type=F32) * scaling
    )
    itself = jnp.einsum("rhd,rd->rh", queried, new_key, preferred_element_type=F32) * scaling
    position = lax.broadcasted_iota(jnp.int32, (1, 1, context), 2)
    cached = jnp.where(position < lengths[:, None, None], cached, -jnp.inf)
    highest = jnp.maximum(jnp.max(cached, axis=2), itself)
    cached_exp = jnp.exp(cached - highest[:, :, None])
    itself_exp = jnp.exp(itself - highest)
    totals = jnp.sum(cached_exp, axis=2) + itself_exp
    cached_probs = (cached_exp / totals[:, :, None]).astype(BF)
    itself_probs = (itself_exp / totals).astype(BF)
    mixture = jnp.einsum("rhp,rpd->rhd", cached_probs, cache_values, preferred_element_type=F32)
    mixture = (
        mixture + itself_probs.astype(F32)[:, :, None] * new_value.astype(F32)[:, None, :]
    )
    return mixture.astype(BF)


VMEM = pl.BlockSpec(memory_space=pltpu.VMEM)
SMEM = pl.BlockSpec(memory_space=pltpu.SMEM)
HBM = pl.BlockSpec(memory_space=pl.ANY)


def at16(index):
    return pl.multiple_of(index, 16)


def project_kernel(place, a0, a1, a2, a3, b0, b1, b2, b3, w, sent, kept, tail, rows):
    z, x = place[0], place[1]
    for k, a in enumerate((a0, a1, a2, a3)):
        for i in range(4):
            row = at16((z - i + 4) % 4 * 64 + (x - k + 4) % 4 * 16)
            rows[pl.ds(row, 16), :KE] = a[16 * i : 16 * i + 16, :KE]
            tail[pl.ds(row, 16), :128] = a[16 * i : 16 * i + 16, KE:]
    for k, b in enumerate((b0, b1, b2, b3)):
        for i in range(4):
            row = at16((z - k + 4) % 4 * 64 + (x - i + 4) % 4 * 16)
            rows[pl.ds(row, 16), KE:] = b[16 * i : 16 * i + 16, :KE]
            tail[pl.ds(row, 16), 128:] = b[16 * i : 16 * i + 16, KE:]
    product = lax.dot_general(
        w[...], rows[...], (((1,), (1,)), ((), ())), preferred_element_type=F32
    )
    kept[...] = product[: 2 * COLS]
    sent[...] = product[2 * COLS :].astype(BF)


def project(place, firsts, seconds, weights):
    return pl.pallas_call(
        project_kernel,
        out_shape=(
            jax.ShapeDtypeStruct((2 * COLS, 256), BF),
            jax.ShapeDtypeStruct((2 * COLS, 256), F32),
            jax.ShapeDtypeStruct((256, 256), BF),
        ),
        in_specs=[SMEM] + [VMEM] * 9,
        out_specs=(VMEM,) * 3,
        scratch_shapes=[pltpu.VMEM((256, KQ), BF)],
        compiler_params=pltpu.CompilerParams(vmem_limit_bytes=24 << 20),
        name="project",
    )(place, *firsts, *seconds, weights)


def mix_kernel(kept, near, other, gain, tail, dispatched):
    projected = kept[...] + near[...].astype(F32) + other[...]
    back = tail[:, :128].astype(F32).T[:COLS]
    widened = (back + projected).astype(BF).astype(F32)
    carried = (widened * gain[...]).astype(BF)
    position = lax.broadcasted_iota(jnp.int32, (256, 128), 0)
    slot = lax.broadcasted_iota(jnp.int32, (256, 128), 1)
    z, x, y, c = position // 64, position // 16 % 4, position // 8 % 2, position // 4 % 2
    here = ((c * 4 + z) * 4 + x) * 2 + y == slot // 2
    rank = (slot % 2 + 1).astype(F32)
    ranks = tail[:, 128:].astype(F32)
    for e in range(EXPERTS):
        pick = jnp.where(here & (ranks[:, e : e + 1] == rank), 1.0, 0.0).astype(BF)
        block = jnp.dot(carried, pick, preferred_element_type=F32).astype(BF)
        for device in range(8):
            dispatched[8 * e + device] = block


def mix(kept, near, other, gain, tail):
    return pl.pallas_call(
        mix_kernel,
        out_shape=jax.ShapeDtypeStruct((64, COLS, 128), BF),
        in_specs=[VMEM] * 5,
        out_specs=VMEM,
        compiler_params=pltpu.CompilerParams(vmem_limit_bytes=12 << 20),
        name="mix",
    )(kept, near, other, gain, tail)


def square_kernel(arrived, inverse, out):
    for g in range(2):
        total = jnp.zeros((8, 128), F32)
        for i in range(32):
            value = arrived[32 * g + i].astype(F32) * inverse[i]
            total = total + jnp.sum((value * value).reshape(14, 8, 128), axis=0)
        out[:, 128 * g : 128 * g + 128] = total


def squares_of(arrived, inverse):
    return pl.pallas_call(
        square_kernel,
        out_shape=jax.ShapeDtypeStruct((8, 256), F32),
        in_specs=[VMEM] * 2,
        out_specs=VMEM,
        compiler_params=pltpu.CompilerParams(vmem_limit_bytes=12 << 20),
        name="squares",
    )(arrived, inverse)


DEPTH = 1024


def expert_kernel(
    place, own, other, own_squares, other_squares, gate, up, sent, kept, resid,
    columns, gates, ups, act, sems,
):
    x, y, c = place[1], place[2], place[3]
    copies = []
    for k in range(D // DEPTH):
        lanes = pl.ds(k * DEPTH, DEPTH)
        copies.append((
            pltpu.make_async_copy(gate.at[:, lanes], gates.at[:, lanes], sems.at[2 * k]),
            pltpu.make_async_copy(up.at[:, lanes], ups.at[:, lanes], sems.at[2 * k + 1]),
        ))
    for pair in copies:
        for copy in pair:
            copy.start()

    for ref, of_c in ((own, c), (other, 1 - c)):
        for i in range(32):
            row = at16((2 * i + of_c) * COLS)
            columns[pl.ds(row, COLS), :128] = ref[i]
            columns[pl.ds(row, COLS), 128:] = ref[32 + i]
    squares = own_squares[...] + other_squares[...]
    scale = lax.rsqrt(jnp.sum(squares, axis=0, keepdims=True) / D + 1e-05)

    gated = jnp.zeros((HID_DEV, 256), F32)
    upward = jnp.zeros((HID_DEV, 256), F32)
    for k, pair in enumerate(copies):
        for copy in pair:
            copy.wait()
        lanes = slice(k * DEPTH, (k + 1) * DEPTH)
        part = columns[lanes, :]
        gated = gated + jnp.dot(gates[:, lanes], part, preferred_element_type=F32)
        upward = upward + jnp.dot(ups[:, lanes], part, preferred_element_type=F32)
    gated = gated * scale
    upward = upward * scale
    activated = gated / (1.0 + jnp.exp(-gated)) * upward
    act[...] = activated.T.astype(BF)
    for g in range(2):
        sent[g * 64 : g * 64 + 64, :] = act[pl.ds(at16(g * 128 + (1 - c) * 64), 64), :]
        kept[g * 64 : g * 64 + 64, :] = act[pl.ds(at16(g * 128 + c * 64), 64), :]
    row = lax.broadcasted_iota(jnp.int32, (128, 256), 0)
    lane = lax.broadcasted_iota(jnp.int32, (128, 256), 1)
    mine = (row // 2 % 8 == x * 2 + y) & (lane == row // 64 * 128 + c * 64 + row % 64)
    resid[...] = lax.dot_general(
        jnp.where(mine, 1.0, 0.0).astype(BF), columns[...],
        (((1,), (1,)), ((), ())), preferred_element_type=F32,
    ).astype(BF)


def expert(place, own, other, own_squares, other_squares, gate, up):
    return pl.pallas_call(
        expert_kernel,
        out_shape=(
            jax.ShapeDtypeStruct((128, HID_DEV), BF),
            jax.ShapeDtypeStruct((128, HID_DEV), BF),
            jax.ShapeDtypeStruct((128, D), BF),
        ),
        in_specs=[SMEM] + [VMEM] * 4 + [HBM] * 2,
        out_specs=(VMEM,) * 3,
        scratch_shapes=[
            pltpu.VMEM((D, 256), BF),
            pltpu.VMEM((HID_DEV, D), BF),
            pltpu.VMEM((HID_DEV, D), BF),
            pltpu.VMEM((256, HID_DEV), BF),
            pltpu.SemaphoreType.DMA((2 * (D // DEPTH),)),
        ],
        compiler_params=pltpu.CompilerParams(vmem_limit_bytes=32 << 20),
        name="expert",
    )(place, own, other, own_squares, other_squares, gate, up)


def lower_kernel(own, other, down, other_down, resid, inverse, out):
    width = D // 4
    for k in range(4):
        lanes = slice(k * width, (k + 1) * width)
        part = jnp.dot(own[...], down[:, lanes], preferred_element_type=F32)
        part = part + jnp.dot(other[...], other_down[:, lanes], preferred_element_type=F32)
        out[:, lanes] = (part + resid[:, lanes].astype(F32) * inverse[:, lanes]).astype(BF)


def lower(own, other, down, other_down, resid, inverse):
    return pl.pallas_call(
        lower_kernel,
        out_shape=jax.ShapeDtypeStruct((128, D), BF),
        in_specs=[VMEM] * 6,
        out_specs=VMEM,
        compiler_params=pltpu.CompilerParams(vmem_limit_bytes=24 << 20),
        name="lower",
    )(own, other, down, other_down, resid, inverse)


def per_device(
    hidden,
    queries,
    new_key,
    new_value,
    cache_keys,
    cache_values,
    lengths,
    out_weight,
    ffn_gain,
    gate_weight,
    up_weight,
    down_weight,
    routes,
    route_gates,
):
    z, x, y, c = (lax.axis_index(a) for a in SECTION)
    chunk = ((z * 4 + x) * 2 + y) * 2 + c
    place = jnp.stack([z, x, y, c]).astype(jnp.int32)

    turned = out_weight.T

    def quarter(of_c, of_y):
        return lax.dynamic_slice_in_dim(turned, of_c * KHALF + of_y * KQ, KQ, 1)

    away = (quarter(0, 1 - y), quarter(1, 1 - y))
    queries, away = lax.optimization_barrier((queries, away))
    far_low = ring_gy(away[0], 1)
    far_high = ring_gy(away[1], -1)
    near = quarter(c, y)
    near_other = shift(quarter(1 - c, y), "c")
    other_down = shift(down_weight, "c")

    expert_ids = lax.broadcasted_iota(jnp.int32, (1, 1, EXPERTS), 2)
    named = routes[:, :, None] == expert_ids
    names = jnp.any(named, axis=1).astype(jnp.int32)
    before = jnp.concatenate(
        [jnp.zeros((1, EXPERTS), jnp.int32), jnp.cumsum(names, axis=0)[:-1]], axis=0
    )
    slot_table = names * (before + 1)
    gate_table = jnp.sum(jnp.where(named, route_gates[:, :, None], 0), axis=1).astype(F32)
    shares = gate_table / jnp.sum(route_gates, axis=1, keepdims=True).astype(F32)
    slot_lanes = jnp.pad(slot_table.astype(BF), ((0, 0), (0, 128 - EXPERTS)))

    hidden_lanes = jnp.pad(
        hidden.reshape(4, 4, 4, 2, 2, COLS).transpose(4, 3, 0, 1, 2, 5),
        ((0, 0),) * 5 + ((0, 128 - COLS),),
    ).reshape(2, 2, 4, 4 * 4 * 128)

    def pick(array, index, dim):
        return lax.dynamic_index_in_dim(array, index, dim, keepdims=False)

    attended = attend(queries, new_key, new_value, cache_keys, cache_values, lengths)
    halves = attended.reshape(4, 2, KHALF)

    def for_core(of_c):
        of_hidden = pick(hidden_lanes, of_c, 0)
        return jnp.concatenate(
            [pick(halves, of_c, 1), slot_lanes, of_hidden[0], of_hidden[1]], axis=1
        )

    block = pair_ordered(for_core(c), shift(for_core(1 - c), "c"), c)
    block = block.reshape(8, KHALF + 128 + 4096)

    def for_y(of_y):
        return jnp.concatenate(
            [
                lax.dynamic_slice_in_dim(block, of_y * KQ, KQ, 1),
                block[:, KHALF : KHALF + 128],
                lax.dynamic_slice_in_dim(block, KHALF + 128 + of_y * 2048, 2048, 1),
            ],
            axis=1,
        )

    block = pair_ordered(for_y(y), shift(for_y(1 - y), "y"), y).reshape(16, KQ + 128 + 2048)
    first, second = block[:, :KE], block[:, KE : KQ + 128]
    tails = block[:, KQ + 128 :]

    def with_tail(of_z):
        own = lax.dynamic_slice_in_dim(tails, of_z % 4 * 512, 512, 1)
        return jnp.concatenate([first, own], axis=1)

    firsts = [with_tail(z)] + [shift(with_tail(z + k), "z", k) for k in (1, 2, 3)]
    firsts, seconds, far_low, far_high = lax.optimization_barrier(
        (firsts, [second] + others4(second, "x"), far_low, far_high)
    )
    far = jnp.where(c == 0, far_low, far_high)
    far_other = shift(jnp.where(c == 0, far_high, far_low), "c")
    weights = jnp.concatenate([near, near_other, far, far_other], axis=0)
    first = jnp.concatenate(firsts, axis=0)
    second = jnp.concatenate(seconds, axis=0)
    tails = first[:, KE:]
    first = first[:, :KE]

    def with_column(of_x):
        own = lax.dynamic_slice_in_dim(tails, of_x % 4 * 128, 128, 1)
        return jnp.concatenate([first, own], axis=1)

    firsts = [with_column(x)] + [shift(with_column(x + k), "x", k) for k in (1, 2, 3)]
    seconds = [second] + others4(second, "z")
    sent, kept, tail = project(place, firsts, seconds, weights)
    near_sum = shift(sent, "y")
    gain = lax.dynamic_slice_in_dim(ffn_gain, chunk * COLS, COLS, 0).reshape(COLS, 1)
    crossing = kept[COLS:] + near_sum[COLS:].astype(F32)
    dispatched = mix(kept[:COLS], near_sum[:COLS], shift(crossing, "c"), gain, tail)
    arrived = lax.all_to_all(dispatched, ("g", "z", "x", "y"), 0, 0, tiled=True)
    other = shift(arrived, "c")
    inverse = 1.0 / ffn_gain
    own_inverse = pick(inverse.reshape(32, 2, COLS), c, 1).reshape(32, COLS, 1)
    own_squares = squares_of(arrived, own_inverse)
    sent, kept, resid = expert(
        place, arrived, other, own_squares, shift(own_squares, "c"),
        gate_weight.T, up_weight.T,
    )
    summed = lower(kept, shift(sent, "c"), down_weight, other_down, resid, inverse.reshape(1, D))
    returned = lax.all_to_all(
        summed.reshape(64, 2, D), ("g", "z", "x", "y"), 0, 0, tiled=True
    )
    returned = jnp.sum(returned.reshape(8, 8, 2, D).astype(F32), axis=1)
    ranks = lax.broadcasted_iota(jnp.int32, (1, 1, 2), 2) + 1
    parts = jnp.where(slot_table[:, :, None] == ranks, shares[:, :, None], 0.0)
    return jnp.sum(parts.reshape(4, 16, 1) * returned.reshape(1, 16, D), axis=1).astype(BF)


def solution(mesh):
    fine = Mesh(mesh.devices.reshape(*SIZES.values()), ALL)
    rows = P(ALL, None)
    return jax.shard_map(
        per_device,
        mesh=fine,
        in_specs=(
            rows,
            rows,
            rows,
            rows,
            P(ALL, None, None),
            P(ALL, None, None),
            P(ALL),
            P(None, SECTION),
            P(),
            P(None, ALL),
            P(None, ALL),
            rows,
            rows,
            rows,
        ),
        out_specs=rows,
        check_vma=False,
    )
```

```python
import math

import jax
import jax.numpy as jnp
from jax import lax
from jax.experimental import pallas as pl
from jax.experimental.pallas import tpu as pltpu
from jax.sharding import Mesh, PartitionSpec as P

D = 7168
HEAD = 256
KALL = 16384
KHALF = KALL // 2
KQ = KHALF // 2
FIRST = 1536
LAST = KQ - FIRST
HID_DEV = 320
COLS = 112
EXPERTS = 8
BF = jnp.bfloat16
F32 = jnp.float32
SIZES = {"g": 2, "z": 4, "x": 4, "y": 2, "c": 2}
ALL = ("g", "z", "x", "y", "c")
SECTION = ("z", "x", "y", "c")


def shift(array, axis, step=1):
    n = SIZES[axis]
    return lax.ppermute(array, axis, [(i, (i + step) % n) for i in range(n)])


def others4(array, axis):
    return [shift(array, axis, 1), shift(array, axis, 2), shift(array, axis, 3)]


def ring_gy(array, step, swap=False):
    pairs = [
        (i * 2 + core, (i + step) % 4 * 2 + (1 - core if swap else core))
        for i in range(4)
        for core in range(2)
    ]
    return lax.ppermute(array, ("g", "y", "c"), pairs)


def crossed(array, stage, step):
    pairs = []
    for z in range(4):
        for x in range(4):
            for c in range(2):
                along_z = c == stage
                to = ((z + step) % 4, x) if along_z else (z, (x + step) % 4)
                pairs.append(((z * 4 + x) * 2 + c, (to[0] * 4 + to[1]) * 2 + c))
    return lax.ppermute(array, ("z", "x", "c"), pairs)


def pair_ordered(own, other, mine):
    return jnp.where(
        mine == 0, jnp.stack([own, other]), jnp.stack([other, own])
    )


VMEM = pl.BlockSpec(memory_space=pltpu.VMEM)
SMEM = pl.BlockSpec(memory_space=pltpu.SMEM)
HBM = pl.BlockSpec(memory_space=pltpu.HBM)


def in_hbm(array):
    return pltpu.with_memory_space_constraint(array, pltpu.HBM)


def row_of(value, row):
    here = lax.broadcasted_iota(jnp.int32, value.shape, 0) == row
    return jnp.sum(jnp.where(here, value, 0.0), axis=0, keepdims=True)


def attend_kernel(
    lengths, q, k, v, new_key, new_value, out, keys, values, fresh_key, fresh_value, sems
):
    rows = q.shape[0]
    fresh = [
        pltpu.make_async_copy(new_key, fresh_key, sems.at[2, 0]),
        pltpu.make_async_copy(new_value, fresh_value, sems.at[2, 1]),
    ]
    copies = [
        [
            pltpu.make_async_copy(source.at[r], kept.at[r], sems.at[i, r])
            for i, (source, kept) in enumerate(((k, keys), (v, values)))
        ]
        for r in range(rows)
    ]
    for copy in fresh + [copies[r][i] for p in range(0, rows, 2) for i in range(2) for r in (p, p + 1)]:
        copy.start()
    scaling = 1.0 / math.sqrt(HEAD)
    for copy in fresh:
        copy.wait()
    own_keys, own_values = fresh_key[...].astype(F32), fresh_value[...].astype(F32)
    for pair in range(0, rows, 2):
        probs, own_probs = [], []
        for r in (pair, pair + 1):
            copies[r][0].wait()
        for r in (pair, pair + 1):
            queried = (q[r].astype(F32) * scaling).astype(BF)
            itself = jnp.sum(
                queried.astype(F32) * row_of(own_keys, r), axis=1, keepdims=True
            )
            cached = lax.dot_general(
                queried, keys[r], (((1,), (1,)), ((), ())), preferred_element_type=F32
            )
            position = lax.broadcasted_iota(jnp.int32, cached.shape, 1)
            cached = jnp.where(position < lengths[r], cached, -jnp.inf)
            highest = jnp.maximum(jnp.max(cached, axis=1, keepdims=True), itself)
            cached_exp = jnp.exp(cached - highest)
            itself_exp = jnp.exp(itself - highest)
            share = 1.0 / (jnp.sum(cached_exp, axis=1, keepdims=True) + itself_exp)
            probs.append((cached_exp * share).astype(BF))
            own_probs.append((itself_exp * share).astype(BF).astype(F32))
        for r in (pair, pair + 1):
            copies[r][1].wait()
        for i, r in enumerate((pair, pair + 1)):
            mixture = jnp.dot(probs[i], values[r], preferred_element_type=F32)
            out[r] = (mixture + own_probs[i] * row_of(own_values, r)).astype(BF)


def attend(queries, new_key, new_value, cache_keys, cache_values, lengths):
    rows, context = cache_keys.shape[0], cache_keys.shape[1]
    heads = queries.shape[1] // HEAD
    return pl.pallas_call(
        attend_kernel,
        out_shape=jax.ShapeDtypeStruct((rows, heads, HEAD), BF),
        in_specs=[SMEM, VMEM, HBM, HBM, HBM, HBM],
        out_specs=VMEM,
        scratch_shapes=[
            pltpu.VMEM((rows, context, HEAD), BF),
            pltpu.VMEM((rows, context, HEAD), BF),
            pltpu.VMEM((rows, HEAD), BF),
            pltpu.VMEM((rows, HEAD), BF),
            pltpu.SemaphoreType.DMA((3, rows)),
        ],
        compiler_params=pltpu.CompilerParams(vmem_limit_bytes=24 << 20),
        cost_estimate=pl.CostEstimate(
            flops=4 * rows * heads * context * HEAD,
            bytes_accessed=4 * rows * context * HEAD,
            transcendentals=rows * heads * context,
        ),
        name="attend",
    )(
        in_hbm(lengths),
        queries.reshape(rows, heads, HEAD),
        in_hbm(cache_keys),
        in_hbm(cache_values),
        in_hbm(new_key),
        in_hbm(new_value),
    )


def at16(index):
    return pl.multiple_of(index, 16)


def cut_kernel(place, turned, near, f0, h0, f1, h1, sems):
    y, c = place[2], place[3]
    lanes = lambda start, size: pl.ds(pl.multiple_of(start, 512), size)
    copies = []
    for n, (of_c, of_y, part, size, out) in enumerate((
        (c, 1 - y, 0, FIRST, f0), (1 - c, 1 - y, 0, FIRST, h0), (1 - c, y, 0, KQ, near),
        (c, 1 - y, FIRST, LAST, f1), (1 - c, 1 - y, FIRST, LAST, h1),
    )):
        source = turned.at[:, lanes(of_c * KHALF + of_y * KQ + part, size)]
        copies.append(pltpu.make_async_copy(source, out, sems.at[n]))
    for copy in copies:
        copy.start()
    for copy in copies:
        copy.wait()


def cut(place, turned):
    return pl.pallas_call(
        cut_kernel,
        out_shape=(jax.ShapeDtypeStruct((COLS, KQ), BF),)
        + (jax.ShapeDtypeStruct((COLS, FIRST), BF),) * 2
        + (jax.ShapeDtypeStruct((COLS, LAST), BF),) * 2,
        in_specs=[SMEM, HBM],
        out_specs=(VMEM,) * 5,
        scratch_shapes=[pltpu.SemaphoreType.DMA((5,))],
        compiler_params=pltpu.CompilerParams(vmem_limit_bytes=16 << 20),
        name="cut",
    )(place, in_hbm(turned))


def spread_kernel(place, b0, b1, b2, b3, o0, o1, o2, o3):
    z, x, c = place[0], place[1], place[3]
    second = jnp.where(c == 0, x, z)
    for i, block in enumerate((b0, b1, b2, b3)):
        rows = slice(16 * i, 16 * i + 16)
        for k, out in enumerate((o0, o1, o2, o3)):
            out[rows, :KQ] = block[:, :KQ]
            lanes = pl.multiple_of(KQ + (second + k) % 4 * 128, 128)
            out[rows, KQ:] = block[:, pl.ds(lanes, 128)]


def spread(place, blocks):
    return pl.pallas_call(
        spread_kernel,
        out_shape=(jax.ShapeDtypeStruct((64, KQ + 128), BF),) * 4,
        in_specs=[SMEM] + [VMEM] * 4,
        out_specs=(VMEM,) * 4,
        compiler_params=pltpu.CompilerParams(vmem_limit_bytes=8 << 20),
        name="spread",
    )(place, *blocks)


def project_kernel(
    place, r0, r1, r2, r3, own, other, f0, f1, h0, h1, sent, kept, tail, w, rows, sems
):
    z, x, y, c = place[0], place[1], place[2], place[3]
    quarter = lambda start: pl.ds(pl.multiple_of(start, KQ), KQ)
    parts = (
        (own.at[:, quarter(c * KHALF + y * KQ)], 0, 0, KQ),
        (other, 1, 0, KQ),
        (f0, 2, 0, FIRST), (f1, 2, FIRST, LAST), (h0, 3, 0, FIRST), (h1, 3, FIRST, LAST),
    )
    copies = [
        pltpu.make_async_copy(
            source, w.at[pl.ds(i * COLS, COLS), pl.ds(start, size)], sems.at[n]
        )
        for n, (source, i, start, size) in enumerate(parts)
    ]
    for copy in copies:
        copy.start()
    for k, block in enumerate((r0, r1, r2, r3)):
        for i in range(4):
            of_z = (z - jnp.where(c == 0, i, k) + 4) % 4
            of_x = (x - jnp.where(c == 0, k, i) + 4) % 4
            row = at16(of_z * 64 + of_x * 16)
            rows[pl.ds(row, 16), :] = block[16 * i : 16 * i + 16, :KQ]
            tail[pl.ds(row, 16), :] = block[16 * i : 16 * i + 16, KQ:]
    for copy in copies:
        copy.wait()
    product = lax.dot_general(
        w[...], rows[...], (((1,), (1,)), ((), ())), preferred_element_type=F32
    )
    kept[...] = product[: 2 * COLS]
    sent[...] = product[2 * COLS :].astype(BF)


def project(place, blocks, own, other, fars):
    return pl.pallas_call(
        project_kernel,
        out_shape=(
            jax.ShapeDtypeStruct((2 * COLS, 256), BF),
            jax.ShapeDtypeStruct((2 * COLS, 256), F32),
            jax.ShapeDtypeStruct((256, 128), BF),
        ),
        in_specs=[SMEM] + [VMEM] * 4 + [HBM] + [pl.BlockSpec(memory_space=pl.ANY)] * 5,
        out_specs=(VMEM,) * 3,
        scratch_shapes=[
            pltpu.VMEM((4 * COLS, KQ), BF),
            pltpu.VMEM((256, KQ), BF),
            pltpu.SemaphoreType.DMA((6,)),
        ],
        compiler_params=pltpu.CompilerParams(vmem_limit_bytes=12 << 20),
        name="project",
    )(place, *blocks, in_hbm(own), other, *fars)


def chunk_kernel(gain, out):
    for i in range(D // COLS):
        out[i : i + 1, :] = gain[:, i * COLS : (i + 1) * COLS]


def chunked(gain):
    return pl.pallas_call(
        chunk_kernel,
        out_shape=jax.ShapeDtypeStruct((D // COLS, COLS), F32),
        in_specs=[VMEM],
        out_specs=VMEM,
        compiler_params=pltpu.CompilerParams(vmem_limit_bytes=2 << 20),
        name="chunked",
    )(gain)


def mix_kernel(place, kept, near, other, gains, tail, dispatched):
    chunk = ((place[0] * 4 + place[1]) * 2 + place[2]) * 2 + place[3]
    projected = kept[...] + near[...].astype(F32) + other[...]
    back = tail[...].astype(F32).T[:COLS]
    widened = (back + projected).astype(BF).astype(F32)
    column = jnp.broadcast_to(row_of(gains[...], chunk), (8, COLS)).T[:, :1]
    carried = (widened * column).astype(BF)
    position = lax.broadcasted_iota(jnp.int32, (256, 128), 0)
    slot = lax.broadcasted_iota(jnp.int32, (256, 128), 1)
    z, x, y, c = position // 64, position // 16 % 4, position // 8 % 2, position // 4 % 2
    here = ((c * 4 + z) * 4 + x) * 2 + y == slot // 2
    rank = (slot % 2 + 1).astype(F32)
    ranks = tail[...].astype(F32)
    for e in range(EXPERTS):
        pick = jnp.where(here & (ranks[:, COLS + e : COLS + e + 1] == rank), 1.0, 0.0).astype(BF)
        block = jnp.dot(carried, pick, preferred_element_type=F32).astype(BF)
        for device in range(8):
            dispatched[8 * e + device] = block


def mix(place, kept, near, other, gains, tail):
    return pl.pallas_call(
        mix_kernel,
        out_shape=jax.ShapeDtypeStruct((64, COLS, 128), BF),
        in_specs=[SMEM] + [VMEM] * 5,
        out_specs=VMEM,
        compiler_params=pltpu.CompilerParams(vmem_limit_bytes=12 << 20),
        name="mix",
    )(place, kept, near, other, gains, tail)


def load_kernel(first, second, out, sems):
    copies = []
    for i, source in enumerate((first, second)):
        for k in range(4):
            lanes = pl.ds(k * (D // 4), D // 4)
            copies.append(pltpu.make_async_copy(
                source.at[:, lanes], out.at[pl.ds(i * HID_DEV, HID_DEV), lanes], sems.at[i, k]
            ))
    for copy in copies:
        copy.start()
    for copy in copies:
        copy.wait()


def load(first, second, name):
    return pl.pallas_call(
        load_kernel,
        out_shape=jax.ShapeDtypeStruct((2 * HID_DEV, D), BF),
        in_specs=[HBM] * 2,
        out_specs=VMEM,
        scratch_shapes=[pltpu.SemaphoreType.DMA((2, 4))],
        compiler_params=pltpu.CompilerParams(vmem_limit_bytes=16 << 20),
        cost_estimate=pl.CostEstimate(
            flops=0, bytes_accessed=8 * HID_DEV * D, transcendentals=0
        ),
        name=name,
    )(in_hbm(first), in_hbm(second))


def squares_of(block, scales, chunk_of_c):
    i, c = chunk_of_c
    scale = jnp.where(c == 0, scales[:, 2 * i : 2 * i + 1], scales[:, 2 * i + 1 : 2 * i + 2])
    value = block.astype(F32) * scale
    return jnp.sum((value * value).reshape(14, 8, 128), axis=0)


def receive_kernel(
    place, arrived, gains, gate, up, columns, squares, kept, sent, weights, sems
):
    x, y, c = place[1], place[2], place[3]
    copies = []
    for i, source in enumerate((gate, up)):
        for k in range(4):
            lanes = pl.ds(k * (D // 4), D // 4)
            copies.append(pltpu.make_async_copy(
                source.at[:, lanes], weights.at[pl.ds(i * HID_DEV, HID_DEV), lanes], sems.at[i, k]
            ))
    for copy in copies:
        copy.start()
    scales = 1.0 / gains[...].T
    for g in range(2):
        total = jnp.zeros((8, 128), F32)
        lanes = slice(128 * g, 128 * g + 128)
        for i in range(32):
            block = arrived[32 * g + i]
            columns[pl.ds(at16((2 * i + c) * COLS), COLS), lanes] = block
            columns[pl.ds(at16((2 * i + 1 - c) * COLS), COLS), lanes] = jnp.zeros_like(block)
            total = total + squares_of(block, scales, (i, c))
        squares[:, lanes] = total
    row = lax.broadcasted_iota(jnp.int32, (32, 256), 0)
    lane = lax.broadcasted_iota(jnp.int32, (32, 256), 1)
    of_c = jnp.where(row < 16, c, 1 - c)
    slot = ((of_c * 4 + row // 2 % 4) * 4 + x) * 2 + y
    mine = lane == row // 8 % 2 * 128 + slot * 2 + row % 2
    residual = lax.dot_general(
        jnp.where(mine, 1.0, 0.0).astype(BF), columns[...],
        (((1,), (1,)), ((), ())), preferred_element_type=F32,
    ).astype(BF)
    kept[...] = residual[:16]
    sent[...] = residual[16:]
    for copy in copies:
        copy.wait()


def receive(place, arrived, gains, gate, up):
    return pl.pallas_call(
        receive_kernel,
        out_shape=(
            jax.ShapeDtypeStruct((D, 256), BF),
            jax.ShapeDtypeStruct((8, 256), F32),
            jax.ShapeDtypeStruct((16, D), BF),
            jax.ShapeDtypeStruct((16, D), BF),
            jax.ShapeDtypeStruct((2 * HID_DEV, D), BF),
        ),
        in_specs=[SMEM] + [VMEM] * 2 + [HBM] * 2,
        out_specs=(VMEM,) * 5,
        scratch_shapes=[pltpu.SemaphoreType.DMA((2, 4))],
        compiler_params=pltpu.CompilerParams(vmem_limit_bytes=16 << 20),
        name="receive",
    )(place, arrived, gains, in_hbm(gate), in_hbm(up))


def expert_kernel(place, seen, other, own_squares, gains, weights, sent, kept, columns, act):
    c = place[3]
    scales = 1.0 / gains[...].T
    other_squares = [jnp.zeros((8, 128), F32)] * 2
    for i in range(32):
        own_rows = pl.ds(at16((2 * i + c) * COLS), COLS)
        other_rows = pl.ds(at16((2 * i + 1 - c) * COLS), COLS)
        columns[own_rows, :] = seen[own_rows, :]
        for g in range(2):
            block = other[32 * g + i]
            columns[other_rows, 128 * g : 128 * g + 128] = block
            other_squares[g] = other_squares[g] + squares_of(block, scales, (i, 1 - c))
    product = jnp.dot(weights[...], columns[...], preferred_element_type=F32)
    squares = own_squares[...] + jnp.concatenate(other_squares, axis=1)
    scale = lax.rsqrt(jnp.sum(squares, axis=0, keepdims=True) / D + 1e-05)
    gated = product[:HID_DEV] * scale
    upward = product[HID_DEV:] * scale
    activated = gated / (1.0 + jnp.exp(-gated)) * upward
    act[...] = activated.T.astype(BF)
    for g in range(2):
        sent[g * 64 : g * 64 + 64, :] = act[pl.ds(at16(g * 128 + (1 - c) * 64), 64), :]
        kept[g * 64 : g * 64 + 64, :] = act[pl.ds(at16(g * 128 + c * 64), 64), :]


def expert(place, seen, other, own_squares, gains, weights):
    return pl.pallas_call(
        expert_kernel,
        out_shape=(jax.ShapeDtypeStruct((128, HID_DEV), BF),) * 2,
        in_specs=[SMEM] + [VMEM] * 5,
        out_specs=(VMEM,) * 2,
        scratch_shapes=[pltpu.VMEM((D, 256), BF), pltpu.VMEM((256, HID_DEV), BF)],
        compiler_params=pltpu.CompilerParams(vmem_limit_bytes=16 << 20),
        name="expert",
    )(place, seen, other, own_squares, gains, weights)


def lower_kernel(place, own, other, weights, kept, taken, gain, out, act):
    x, y = place[1], place[2]
    act[:, :HID_DEV] = own[...]
    act[:, HID_DEV:] = other[...]
    row = lax.broadcasted_iota(jnp.int32, (128, 16), 0)
    column = lax.broadcasted_iota(jnp.int32, (128, 16), 1)
    here = (row // 2 % 8 == x * 2 + y) & (row // 16 * 2 + row % 2 == column)
    place_in = jnp.where(here, 1.0, 0.0).astype(BF)
    width = D // 4
    for k in range(4):
        lanes = slice(k * width, (k + 1) * width)
        part = jnp.dot(act[...], weights[:, lanes], preferred_element_type=F32)
        residual = (kept[:, lanes] + taken[:, lanes]).astype(F32) / gain[:, lanes]
        high = residual.astype(BF)
        low = (residual - high.astype(F32)).astype(BF)
        part = part + jnp.dot(place_in, high, preferred_element_type=F32)
        part = part + jnp.dot(place_in, low, preferred_element_type=F32)
        out[:, :, lanes] = part.astype(BF).reshape(64, 2, width)


def lower(place, own, other, weights, kept, taken, gain):
    return pl.pallas_call(
        lower_kernel,
        out_shape=jax.ShapeDtypeStruct((64, 2, D), BF),
        in_specs=[SMEM] + [VMEM] * 6,
        out_specs=VMEM,
        scratch_shapes=[pltpu.VMEM((128, 2 * HID_DEV), BF)],
        compiler_params=pltpu.CompilerParams(vmem_limit_bytes=16 << 20),
        name="lower",
    )(place, own, other, weights, kept, taken, gain)


def combine_kernel(returned, parts, out):
    width = D // 4
    weights = parts[...]
    high = weights.astype(BF)
    low = (weights - high.astype(F32)).astype(BF)
    both = jnp.concatenate([high.astype(F32), low.astype(F32)], axis=0).astype(BF)
    for k in range(4):
        lanes = slice(k * width, (k + 1) * width)
        rows = returned[:, :, lanes].reshape(128, width)
        total = jnp.dot(both, rows, preferred_element_type=F32)
        out[:, lanes] = (total[:4] + total[8:12]).astype(BF)


def combine(returned, parts):
    return pl.pallas_call(
        combine_kernel,
        out_shape=jax.ShapeDtypeStruct((4, D), BF),
        in_specs=[VMEM] * 2,
        out_specs=VMEM,
        compiler_params=pltpu.CompilerParams(vmem_limit_bytes=8 << 20),
        name="combine",
    )(returned, parts)


def per_device(
    hidden,
    queries,
    new_key,
    new_value,
    cache_keys,
    cache_values,
    lengths,
    out_weight,
    ffn_gain,
    gate_weight,
    up_weight,
    down_weight,
    routes,
    route_gates,
):
    z, x, y, c = (lax.axis_index(a) for a in SECTION)
    chunk = ((z * 4 + x) * 2 + y) * 2 + c
    place = jnp.stack([z, x, y, c]).astype(jnp.int32)

    turned = out_weight.T

    expert_ids = lax.broadcasted_iota(jnp.int32, (1, 1, EXPERTS), 2)
    named = routes[:, :, None] == expert_ids
    names = jnp.any(named, axis=1).astype(jnp.int32)
    before = jnp.concatenate(
        [jnp.zeros((1, EXPERTS), jnp.int32), jnp.cumsum(names, axis=0)[:-1]], axis=0
    )
    slot_table = names * (before + 1)
    gate_table = jnp.sum(jnp.where(named, route_gates[:, :, None], 0), axis=1).astype(F32)
    shares = gate_table / jnp.sum(route_gates, axis=1, keepdims=True).astype(F32)
    ranks = lax.broadcasted_iota(jnp.int32, (1, 1, 8, 2), 3) + 1
    parts = jnp.where(
        slot_table[:, :, None, None] == ranks, shares[:, :, None, None], 0.0
    ).reshape(4, 128)
    parts = jnp.pad(parts, ((0, 4), (0, 0)))
    slot_lanes = jnp.pad(slot_table.astype(BF), ((0, 0), (0, 8)))

    def pick(array, index, dim):
        return lax.dynamic_index_in_dim(array, index, dim, keepdims=False)

    tails = jnp.concatenate(
        [
            hidden.reshape(4, 32, 2, COLS).transpose(2, 0, 1, 3),
            jnp.broadcast_to(slot_lanes[None, :, None, :], (2, 4, 32, 16)),
        ],
        axis=3,
    ).reshape(2, 4, 4, 4, 2, 128)
    tails = jnp.stack(
        [tails[0].transpose(3, 0, 1, 2, 4), tails[1].transpose(3, 0, 2, 1, 4)]
    ).reshape(2, 2, 4, 16 * 128)

    other_down = shift(down_weight, "c")
    attended = attend(queries, new_key, new_value, cache_keys, cache_values, lengths)
    halves = attended.reshape(4, 2, KHALF)

    def for_core(of_c):
        of_tails = pick(tails, of_c, 0)
        return jnp.concatenate([pick(halves, of_c, 1), of_tails[0], of_tails[1]], axis=1)

    block = pair_ordered(for_core(c), shift(for_core(1 - c), "c"), c).reshape(8, KHALF + 4096)
    block, cuttable = lax.optimization_barrier((block, turned))
    near, f0, h0, f1, h1 = cut(place, cuttable)
    near = shift(near, "c")

    def for_y(of_y):
        return jnp.concatenate(
            [
                lax.dynamic_slice_in_dim(block, of_y * KQ, KQ, 1),
                lax.dynamic_slice_in_dim(block, KHALF + of_y * 2048, 2048, 1),
            ],
            axis=1,
        )

    block = pair_ordered(for_y(y), shift(for_y(1 - y), "y"), y).reshape(16, KQ + 2048)
    block, f0, h0 = lax.optimization_barrier((block, f0, h0))
    f0, h0 = ring_gy(f0, 1), ring_gy(h0, -1, True)
    block, near, other_down = lax.optimization_barrier((block, near, other_down))
    along = jnp.where(c == 0, z, x)

    def with_tail(k):
        own = lax.dynamic_slice_in_dim(block, KQ + (along + k) % 4 * 512, 512, 1)
        return jnp.concatenate([block[:, :KQ], own], axis=1)

    blocks = [with_tail(0)] + [crossed(with_tail(k), 0, k) for k in (1, 2, 3)]
    blocks, f0, h0, f1, h1 = lax.optimization_barrier((blocks, f0, h0, f1, h1))
    f1, h1 = ring_gy(f1, 1), ring_gy(h1, -1, True)
    blocks, ffn_gain = lax.optimization_barrier((spread(place, blocks), ffn_gain))
    ffn_gain = ffn_gain.reshape(1, D)
    gains = chunked(ffn_gain)
    blocks = [blocks[0]] + [crossed(blocks[k], 1, k) for k in (1, 2, 3)]
    blocks, gains = lax.optimization_barrier((blocks, gains))
    sent, kept, tail = project(
        place, blocks, turned, near, (f0, f1, h0, h1)
    )
    near_sum = shift(sent, "y")
    crossing = kept[COLS:] + near_sum[COLS:].astype(F32)
    dispatched = mix(
        place, kept[:COLS], near_sum[:COLS], shift(crossing, "c"), gains, tail
    )
    dispatched, ready = lax.optimization_barrier((dispatched, (down_weight, other_down)))
    lower_weights = load(*ready, "load_lower")
    arrived = lax.all_to_all(dispatched, ("g", "z", "x", "y"), 0, 0, tiled=True)
    arrived, lower_weights = lax.optimization_barrier((arrived, lower_weights))
    other = shift(arrived, "c")
    seen, squares, kept, sent, upper_weights = receive(
        place, arrived, gains, gate_weight.T, up_weight.T
    )
    taken = shift(sent, "c")
    sent, own = expert(place, seen, other, squares, gains, upper_weights)
    summed = lower(place, own, shift(sent, "c"), lower_weights, kept, taken, ffn_gain)
    returned = lax.all_to_all(summed, ("g", "z", "x", "y"), 0, 0, tiled=True)
    return combine(returned, parts)


def solution(mesh):
    fine = Mesh(mesh.devices.reshape(*SIZES.values()), ALL)
    rows = P(ALL, None)
    return jax.shard_map(
        per_device,
        mesh=fine,
        in_specs=(
            rows,
            rows,
            rows,
            rows,
            P(ALL, None, None),
            P(ALL, None, None),
            P(ALL),
            P(None, SECTION),
            P(),
            P(None, ALL),
            P(None, ALL),
            rows,
            rows,
            rows,
        ),
        out_specs=rows,
        check_vma=False,
    )
```

```python
import math

import jax
import jax.numpy as jnp
from jax import lax
from jax.experimental import pallas as pl
from jax.experimental.pallas import tpu as pltpu
from jax.sharding import Mesh, PartitionSpec as P

D = 7168
HEAD = 256
KALL = 16384
KHALF = KALL // 2
KQ = KHALF // 2
HID_DEV = 320
COLS = 112
EXPERTS = 8
BF = jnp.bfloat16
F32 = jnp.float32
SIZES = {"g": 2, "z": 4, "x": 4, "y": 2, "c": 2}
ALL = ("g", "z", "x", "y", "c")
SECTION = ("z", "x", "y", "c")


def shift(array, axis, step=1):
    n = SIZES[axis]
    return lax.ppermute(array, axis, [(i, (i + step) % n) for i in range(n)])


def others4(array, axis):
    return [shift(array, axis, 1), shift(array, axis, 2), shift(array, axis, 3)]


def ring_gy(array, step, swap=False):
    pairs = [
        (i * 2 + core, (i + step) % 4 * 2 + (1 - core if swap else core))
        for i in range(4)
        for core in range(2)
    ]
    return lax.ppermute(array, ("g", "y", "c"), pairs)


def around(array, k):
    return lax.ppermute(array, ("y", "c"), [(i, i ^ k) for i in range(4)])


def crossed(array, stage, step):
    pairs = []
    for z in range(4):
        for x in range(4):
            for c in range(2):
                along_z = c == stage
                to = ((z + step) % 4, x) if along_z else (z, (x + step) % 4)
                pairs.append(((z * 4 + x) * 2 + c, (to[0] * 4 + to[1]) * 2 + c))
    return lax.ppermute(array, ("z", "x", "c"), pairs)


def pair_ordered(own, other, mine):
    return jnp.where(
        mine == 0, jnp.stack([own, other]), jnp.stack([other, own])
    )


VMEM = pl.BlockSpec(memory_space=pltpu.VMEM)
SMEM = pl.BlockSpec(memory_space=pltpu.SMEM)
HBM = pl.BlockSpec(memory_space=pltpu.HBM)


def in_hbm(array):
    return pltpu.with_memory_space_constraint(array, pltpu.HBM)


def row_of(value, row):
    here = lax.broadcasted_iota(jnp.int32, value.shape, 0) == row
    return jnp.sum(jnp.where(here, value, 0.0), axis=0, keepdims=True)


def attend_kernel(
    lengths, routes, route_gates, place, q_in, hidden_in, k, v, new_key, new_value, turned,
    p0, p1, p2, p3, f0, h0, near, parts,
    q, hidden, keys, values, fresh_key, fresh_value, heads_of, flat, tails, sems,
):
    rows = q.shape[0]
    y, c = place[2], place[3]
    fresh = [
        pltpu.make_async_copy(q_in, q, sems.at[2, 0]),
        pltpu.make_async_copy(hidden_in, hidden, sems.at[2, 1]),
        pltpu.make_async_copy(new_key, fresh_key, sems.at[2, 2]),
        pltpu.make_async_copy(new_value, fresh_value, sems.at[2, 3]),
    ]
    cuts = []
    for n, (of_c, of_y, part) in enumerate(((c, 1 - y, f0), (1 - c, 1 - y, h0), (1 - c, y, near))):
        at = pl.multiple_of(of_c * KHALF + of_y * KQ, KQ)
        cuts.append(pltpu.make_async_copy(
            turned.at[:, pl.ds(at, KQ)], part, sems.at[3, n]
        ))
    copies = [
        [
            pltpu.make_async_copy(source.at[r], kept.at[r], sems.at[i, r])
            for i, (source, kept) in enumerate(((k, keys), (v, values)))
        ]
        for r in range(rows)
    ]
    for copy in fresh + [copies[r][i] for p in range(0, rows, 2) for i in range(2) for r in (p, p + 1)]:
        copy.start()
    for copy in cuts:
        copy.start()
    fresh[0].wait()
    scaling = 1.0 / math.sqrt(HEAD)
    scaled = q[...].astype(F32) * scaling
    for h in range(heads_of.shape[1]):
        heads_of[:, h, :] = scaled[:, h * HEAD : (h + 1) * HEAD]

    lane = lax.broadcasted_iota(jnp.int32, (1, 128), 1) - COLS
    line = lax.broadcasted_iota(jnp.int32, (rows, 128), 0)
    count = jnp.zeros((1, 128), F32)
    slots = jnp.zeros((rows, 128), F32)
    for r in range(rows):
        named = (lane == routes[r, 0]) | (lane == routes[r, 1]) | (lane == routes[r, 2])
        count = count + jnp.where(named, 1.0, 0.0)
        slots = slots + jnp.where((line == r) & named, count, 0.0)
    spot = lax.broadcasted_iota(jnp.int32, (1, 128), 1)
    half = lax.broadcasted_iota(jnp.int32, (2 * rows, 128), 0)
    of_expert, of_slot = spot // 16, spot % 2
    used = jnp.zeros((1, 128), jnp.int32)
    combined = jnp.zeros((2 * rows, 128), F32)
    for r in range(rows):
        gates = [jnp.full((1, 128), route_gates[r, k], jnp.int32).astype(F32) for k in range(3)]
        named = [of_expert == routes[r, k] for k in range(3)]
        chosen = jnp.zeros((1, 128), F32)
        for k in range(3):
            chosen = chosen + jnp.where(named[k], gates[k], 0.0)
        share = chosen / (gates[0] + gates[1] + gates[2])
        here = named[0] | named[1] | named[2]
        share = jnp.where(here & (used == of_slot), share, 0.0)
        used = used + jnp.where(here, 1, 0)
        high = share.astype(BF).astype(F32)
        combined = combined + jnp.where(half == r, high, 0.0)
        combined = combined + jnp.where(half == rows + r, share - high, 0.0)
    parts[...] = combined.astype(BF)
    fresh[1].wait()
    stream = hidden[...].astype(F32)
    blank = jnp.zeros((rows, 128 - COLS), F32)
    for z in range(4):
        for x in range(4):
            for iy in range(2):
                for ic in range(2):
                    chunk = ((z * 4 + x) * 2 + iy) * 2 + ic
                    at = (x * 4 + z if ic else z * 4 + x) * 128
                    part = stream[:, chunk * COLS : (chunk + 1) * COLS]
                    part = jnp.concatenate([part, blank], axis=1) + slots
                    tails[ic * 2 + iy, :, at : at + 128] = part.astype(BF)

    for copy in fresh[2:]:
        copy.wait()
    own_keys, own_values = fresh_key[...].astype(F32), fresh_value[...].astype(F32)
    for pair in range(0, rows, 2):
        probs, own_probs = [], []
        for r in (pair, pair + 1):
            copies[r][0].wait()
        for r in (pair, pair + 1):
            queried = heads_of[r]
            itself = jnp.sum(queried * row_of(own_keys, r), axis=1, keepdims=True)
            cached = lax.dot_general(
                queried.astype(BF), keys[r], (((1,), (1,)), ((), ())),
                preferred_element_type=F32,
            )
            position = lax.broadcasted_iota(jnp.int32, cached.shape, 1)
            cached = jnp.where(position < lengths[r], cached, -jnp.inf)
            highest = jnp.maximum(jnp.max(cached, axis=1, keepdims=True), itself)
            cached_exp = jnp.exp(cached - highest)
            itself_exp = jnp.exp(itself - highest)
            share = 1.0 / (jnp.sum(cached_exp, axis=1, keepdims=True) + itself_exp)
            probs.append((cached_exp * share).astype(BF))
            own_probs.append((itself_exp * share).astype(BF).astype(F32))
        for r in (pair, pair + 1):
            copies[r][1].wait()
        for i, r in enumerate((pair, pair + 1)):
            mixture = jnp.dot(probs[i], values[r], preferred_element_type=F32)
            mixture = mixture + own_probs[i] * row_of(own_values, r)
            for h in range(mixture.shape[0]):
                at = h % 16 * HEAD
                flat[h // 16, r : r + 1, at : at + HEAD] = mixture[h : h + 1, :]
    for k, out in enumerate((p0, p1, p2, p3)):
        of_c = 1 - c if k % 2 else c
        of_y = 1 - y if k // 2 else y
        out[:, :KQ] = flat[of_c * 2 + of_y].astype(BF)
        out[:, KQ:] = tails[of_c * 2 + of_y]
    for copy in cuts:
        copy.wait()


def attend(
    queries, new_key, new_value, cache_keys, cache_values, lengths, routes, route_gates, hidden,
    place, turned,
):
    rows, context = cache_keys.shape[0], cache_keys.shape[1]
    heads = queries.shape[1] // HEAD
    return pl.pallas_call(
        attend_kernel,
        out_shape=(
            *(jax.ShapeDtypeStruct((rows, KQ + 16 * 128), BF),) * 4,
            jax.ShapeDtypeStruct((COLS, KQ), BF),
            jax.ShapeDtypeStruct((COLS, KQ), BF),
            jax.ShapeDtypeStruct((COLS, KQ), BF),
            jax.ShapeDtypeStruct((2 * rows, 128), BF),
        ),
        in_specs=[SMEM] * 4 + [HBM] * 7,
        out_specs=(VMEM,) * 8,
        scratch_shapes=[
            pltpu.VMEM(queries.shape, BF),
            pltpu.VMEM(hidden.shape, BF),
            pltpu.VMEM((rows, context, HEAD), BF),
            pltpu.VMEM((rows, context, HEAD), BF),
            pltpu.VMEM((rows, HEAD), BF),
            pltpu.VMEM((rows, HEAD), BF),
            pltpu.VMEM((rows, heads, HEAD), F32),
            pltpu.VMEM((4, rows, KQ), F32),
            pltpu.VMEM((4, rows, 16 * 128), BF),
            pltpu.SemaphoreType.DMA((4, rows)),
        ],
        compiler_params=pltpu.CompilerParams(vmem_limit_bytes=24 << 20),
        cost_estimate=pl.CostEstimate(
            flops=4 * rows * heads * context * HEAD,
            bytes_accessed=4 * rows * context * HEAD,
            transcendentals=rows * heads * context,
        ),
        name="attend",
    )(
        in_hbm(lengths),
        in_hbm(routes),
        in_hbm(route_gates),
        place,
        in_hbm(queries),
        in_hbm(hidden),
        in_hbm(cache_keys),
        in_hbm(cache_values),
        in_hbm(new_key),
        in_hbm(new_value),
        in_hbm(turned),
    )


def at16(index):
    return pl.multiple_of(index, 16)


def spread_kernel(place, b0, b1, b2, b3, o0, o1, o2, o3):
    z, x, c = place[0], place[1], place[3]
    second = jnp.where(c == 0, x, z)
    for i, block in enumerate((b0, b1, b2, b3)):
        rows = slice(16 * i, 16 * i + 16)
        for k, out in enumerate((o0, o1, o2, o3)):
            out[rows, :KQ] = block[:, :KQ]
            lanes = pl.multiple_of(KQ + (second + k) % 4 * 128, 128)
            out[rows, KQ:] = block[:, pl.ds(lanes, 128)]


def spread(place, blocks):
    return pl.pallas_call(
        spread_kernel,
        out_shape=(jax.ShapeDtypeStruct((64, KQ + 128), BF),) * 4,
        in_specs=[SMEM] + [VMEM] * 4,
        out_specs=(VMEM,) * 4,
        compiler_params=pltpu.CompilerParams(vmem_limit_bytes=8 << 20),
        name="spread",
    )(place, *blocks)


def project_kernel(
    place, r0, r1, r2, r3, own, other, far, far_other, kept, s1, s2, s3, tail, w, rows, sems
):
    z, x, y, c = place[0], place[1], place[2], place[3]
    quarter = lambda start: pl.ds(pl.multiple_of(start, KQ), KQ)
    sources = (own.at[:, quarter(c * KHALF + y * KQ)], other, far, far_other)
    copies = [
        pltpu.make_async_copy(source, w.at[pl.ds(n * COLS, COLS), :], sems.at[n])
        for n, source in enumerate(sources)
    ]
    for copy in copies:
        copy.start()
    for k, block in enumerate((r0, r1, r2, r3)):
        for i in range(4):
            of_z = (z - jnp.where(c == 0, i, k) + 4) % 4
            of_x = (x - jnp.where(c == 0, k, i) + 4) % 4
            row = at16(of_z * 64 + of_x * 16)
            rows[pl.ds(row, 16), :] = block[16 * i : 16 * i + 16, :KQ]
            tail[pl.ds(row, 16), :] = block[16 * i : 16 * i + 16, KQ:]
    for copy in copies:
        copy.wait()
    product = lax.dot_general(
        w[...], rows[...], (((1,), (1,)), ((), ())), preferred_element_type=F32
    )
    kept[...] = product[:COLS]
    for i, sent in enumerate((s1, s2, s3)):
        sent[...] = product[(i + 1) * COLS : (i + 2) * COLS].astype(BF)


def project(place, blocks, own, other, fars):
    return pl.pallas_call(
        project_kernel,
        out_shape=(
            jax.ShapeDtypeStruct((COLS, 256), F32),
            *(jax.ShapeDtypeStruct((COLS, 256), BF),) * 3,
            jax.ShapeDtypeStruct((256, 128), BF),
        ),
        in_specs=[SMEM] + [VMEM] * 4 + [HBM] + [pl.BlockSpec(memory_space=pl.ANY)] * 3,
        out_specs=(VMEM,) * 5,
        scratch_shapes=[
            pltpu.VMEM((4 * COLS, KQ), BF),
            pltpu.VMEM((256, KQ), BF),
            pltpu.SemaphoreType.DMA((4,)),
        ],
        compiler_params=pltpu.CompilerParams(vmem_limit_bytes=12 << 20),
        name="project",
    )(place, *blocks, in_hbm(own), other, *fars)


def chunk_kernel(gain, out):
    for i in range(D // COLS):
        out[i : i + 1, :] = gain[:, i * COLS : (i + 1) * COLS]


def chunked(gain):
    return pl.pallas_call(
        chunk_kernel,
        out_shape=jax.ShapeDtypeStruct((D // COLS, COLS), F32),
        in_specs=[VMEM],
        out_specs=VMEM,
        compiler_params=pltpu.CompilerParams(vmem_limit_bytes=2 << 20),
        name="chunked",
    )(gain)


def mix_kernel(place, kept, r1, r2, r3, gains, tail, dispatched):
    chunk = ((place[0] * 4 + place[1]) * 2 + place[2]) * 2 + place[3]
    projected = kept[...] + r1[...].astype(F32) + (r2[...].astype(F32) + r3[...].astype(F32))
    back = tail[...].astype(F32).T[:COLS]
    widened = (back + projected).astype(BF).astype(F32)
    column = jnp.broadcast_to(row_of(gains[...], chunk), (8, COLS)).T[:, :1]
    carried = (widened * column).astype(BF)
    position = lax.broadcasted_iota(jnp.int32, (256, 128), 0)
    slot = lax.broadcasted_iota(jnp.int32, (256, 128), 1)
    z, x, y, c = position // 64, position // 16 % 4, position // 8 % 2, position // 4 % 2
    here = ((c * 4 + z) * 4 + x) * 2 + y == slot // 2
    rank = (slot % 2 + 1).astype(F32)
    ranks = tail[...].astype(F32)
    for e in range(EXPERTS):
        pick = jnp.where(here & (ranks[:, COLS + e : COLS + e + 1] == rank), 1.0, 0.0).astype(BF)
        block = jnp.dot(carried, pick, preferred_element_type=F32).astype(BF)
        for device in range(8):
            dispatched[8 * e + device] = block


def mix(place, kept, taken, gains, tail):
    return pl.pallas_call(
        mix_kernel,
        out_shape=jax.ShapeDtypeStruct((64, COLS, 128), BF),
        in_specs=[SMEM] + [VMEM] * 6,
        out_specs=VMEM,
        compiler_params=pltpu.CompilerParams(vmem_limit_bytes=12 << 20),
        name="mix",
    )(place, kept, *taken, gains, tail)


def load_kernel(first, second, out, sems):
    copies = []
    for i, source in enumerate((first, second)):
        for k in range(4):
            lanes = pl.ds(k * (D // 4), D // 4)
            copies.append(pltpu.make_async_copy(
                source.at[:, lanes], out.at[pl.ds(i * HID_DEV, HID_DEV), lanes], sems.at[i, k]
            ))
    for copy in copies:
        copy.start()
    for copy in copies:
        copy.wait()


def load(first, second, name):
    return pl.pallas_call(
        load_kernel,
        out_shape=jax.ShapeDtypeStruct((2 * HID_DEV, D), BF),
        in_specs=[HBM] * 2,
        out_specs=VMEM,
        scratch_shapes=[pltpu.SemaphoreType.DMA((2, 4))],
        compiler_params=pltpu.CompilerParams(vmem_limit_bytes=16 << 20),
        cost_estimate=pl.CostEstimate(
            flops=0, bytes_accessed=8 * HID_DEV * D, transcendentals=0
        ),
        name=name,
    )(in_hbm(first), in_hbm(second))


def squares_of(block, scales, chunk_of_c):
    i, c = chunk_of_c
    scale = jnp.where(c == 0, scales[:, 2 * i : 2 * i + 1], scales[:, 2 * i + 1 : 2 * i + 2])
    value = block.astype(F32) * scale
    return jnp.sum((value * value).reshape(14, 8, 128), axis=0)


def receive_kernel(
    place, arrived, gains, gate, up, columns, squares, kept, sent, weights, sems
):
    x, y, c = place[1], place[2], place[3]
    copies = []
    for i, source in enumerate((gate, up)):
        for k in range(4):
            lanes = pl.ds(k * (D // 4), D // 4)
            copies.append(pltpu.make_async_copy(
                source.at[:, lanes], weights.at[pl.ds(i * HID_DEV, HID_DEV), lanes], sems.at[i, k]
            ))
    for copy in copies:
        copy.start()
    scales = 1.0 / gains[...].T
    for g in range(2):
        total = jnp.zeros((8, 128), F32)
        lanes = slice(128 * g, 128 * g + 128)
        for i in range(32):
            block = arrived[32 * g + i]
            columns[pl.ds(at16((2 * i + c) * COLS), COLS), lanes] = block
            columns[pl.ds(at16((2 * i + 1 - c) * COLS), COLS), lanes] = jnp.zeros_like(block)
            total = total + squares_of(block, scales, (i, c))
        squares[:, lanes] = total
    row = lax.broadcasted_iota(jnp.int32, (32, 256), 0)
    lane = lax.broadcasted_iota(jnp.int32, (32, 256), 1)
    of_c = jnp.where(row < 16, c, 1 - c)
    slot = ((of_c * 4 + row // 2 % 4) * 4 + x) * 2 + y
    mine = lane == row // 8 % 2 * 128 + slot * 2 + row % 2
    residual = lax.dot_general(
        jnp.where(mine, 1.0, 0.0).astype(BF), columns[...],
        (((1,), (1,)), ((), ())), preferred_element_type=F32,
    ).astype(BF)
    kept[...] = residual[:16]
    sent[...] = residual[16:]
    for copy in copies:
        copy.wait()


def receive(place, arrived, gains, gate, up):
    return pl.pallas_call(
        receive_kernel,
        out_shape=(
            jax.ShapeDtypeStruct((D, 256), BF),
            jax.ShapeDtypeStruct((8, 256), F32),
            jax.ShapeDtypeStruct((16, D), BF),
            jax.ShapeDtypeStruct((16, D), BF),
            jax.ShapeDtypeStruct((2 * HID_DEV, D), BF),
        ),
        in_specs=[SMEM] + [VMEM] * 2 + [HBM] * 2,
        out_specs=(VMEM,) * 5,
        scratch_shapes=[pltpu.SemaphoreType.DMA((2, 4))],
        compiler_params=pltpu.CompilerParams(vmem_limit_bytes=16 << 20),
        name="receive",
    )(place, arrived, gains, in_hbm(gate), in_hbm(up))


def expert_kernel(place, seen, other, own_squares, gains, weights, sent, kept, columns, act):
    c = place[3]
    scales = 1.0 / gains[...].T
    other_squares = [jnp.zeros((8, 128), F32)] * 2
    for i in range(32):
        own_rows = pl.ds(at16((2 * i + c) * COLS), COLS)
        other_rows = pl.ds(at16((2 * i + 1 - c) * COLS), COLS)
        columns[own_rows, :] = seen[own_rows, :]
        for g in range(2):
            block = other[32 * g + i]
            columns[other_rows, 128 * g : 128 * g + 128] = block
            other_squares[g] = other_squares[g] + squares_of(block, scales, (i, 1 - c))
    product = jnp.dot(weights[...], columns[...], preferred_element_type=F32)
    squares = own_squares[...] + jnp.concatenate(other_squares, axis=1)
    scale = lax.rsqrt(jnp.sum(squares, axis=0, keepdims=True) / D + 1e-05)
    gated = product[:HID_DEV] * scale
    upward = product[HID_DEV:] * scale
    activated = gated / (1.0 + jnp.exp(-gated)) * upward
    act[...] = activated.T.astype(BF)
    for g in range(2):
        sent[g * 64 : g * 64 + 64, :] = act[pl.ds(at16(g * 128 + (1 - c) * 64), 64), :]
        kept[g * 64 : g * 64 + 64, :] = act[pl.ds(at16(g * 128 + c * 64), 64), :]


def expert(place, seen, other, own_squares, gains, weights):
    return pl.pallas_call(
        expert_kernel,
        out_shape=(jax.ShapeDtypeStruct((128, HID_DEV), BF),) * 2,
        in_specs=[SMEM] + [VMEM] * 5,
        out_specs=(VMEM,) * 2,
        scratch_shapes=[pltpu.VMEM((D, 256), BF), pltpu.VMEM((256, HID_DEV), BF)],
        compiler_params=pltpu.CompilerParams(vmem_limit_bytes=16 << 20),
        name="expert",
    )(place, seen, other, own_squares, gains, weights)


def lower_kernel(place, own, other, weights, kept, taken, gain, out, act):
    x, y = place[1], place[2]
    act[:, :HID_DEV] = own[...]
    act[:, HID_DEV:] = other[...]
    row = lax.broadcasted_iota(jnp.int32, (128, 16), 0)
    column = lax.broadcasted_iota(jnp.int32, (128, 16), 1)
    here = (row // 2 % 8 == x * 2 + y) & (row // 16 * 2 + row % 2 == column)
    place_in = jnp.where(here, 1.0, 0.0).astype(BF)
    width = D // 4
    for k in range(4):
        lanes = slice(k * width, (k + 1) * width)
        part = jnp.dot(act[...], weights[:, lanes], preferred_element_type=F32)
        residual = (kept[:, lanes] + taken[:, lanes]).astype(F32) / gain[:, lanes]
        high = residual.astype(BF)
        low = (residual - high.astype(F32)).astype(BF)
        part = part + jnp.dot(place_in, high, preferred_element_type=F32)
        part = part + jnp.dot(place_in, low, preferred_element_type=F32)
        out[:, :, lanes] = part.astype(BF).reshape(64, 2, width)


def lower(place, own, other, weights, kept, taken, gain):
    return pl.pallas_call(
        lower_kernel,
        out_shape=jax.ShapeDtypeStruct((64, 2, D), BF),
        in_specs=[SMEM] + [VMEM] * 6,
        out_specs=VMEM,
        scratch_shapes=[pltpu.VMEM((128, 2 * HID_DEV), BF)],
        compiler_params=pltpu.CompilerParams(vmem_limit_bytes=16 << 20),
        name="lower",
    )(place, own, other, weights, kept, taken, gain)


def combine_kernel(returned, weights, out):
    rows = out.shape[0]
    width = D // 4
    for k in range(4):
        lanes = slice(k * width, (k + 1) * width)
        sums = returned[:, :, lanes].reshape(128, width)
        total = jnp.dot(weights[...], sums, preferred_element_type=F32)
        out[:, lanes] = (total[:rows] + total[rows:]).astype(BF)


def combine(returned, weights):
    return pl.pallas_call(
        combine_kernel,
        out_shape=jax.ShapeDtypeStruct((weights.shape[0] // 2, D), BF),
        in_specs=[VMEM] * 2,
        out_specs=VMEM,
        compiler_params=pltpu.CompilerParams(vmem_limit_bytes=8 << 20),
        name="combine",
    )(returned, weights)


def per_device(
    hidden,
    queries,
    new_key,
    new_value,
    cache_keys,
    cache_values,
    lengths,
    out_weight,
    ffn_gain,
    gate_weight,
    up_weight,
    down_weight,
    routes,
    route_gates,
):
    z, x, y, c = (lax.axis_index(a) for a in SECTION)
    chunk = ((z * 4 + x) * 2 + y) * 2 + c
    place = jnp.stack([z, x, y, c]).astype(jnp.int32)

    turned = out_weight.T

    other_down = shift(down_weight, "c")
    *payloads, f0, h0, near, parts = attend(
        queries, new_key, new_value, cache_keys, cache_values, lengths, routes, route_gates,
        hidden, place, turned,
    )
    near = shift(near, "c")
    far, far_other, near, other_down = lax.optimization_barrier((f0, h0, near, other_down))
    far, far_other = ring_gy(far, 1), ring_gy(far_other, -1, True)
    got = [payloads[0]] + [around(payloads[k], k) for k in (1, 2, 3)]
    block = pair_ordered(pair_ordered(got[0], got[1], c), pair_ordered(got[2], got[3], c), y)
    block = block.reshape(16, KQ + 2048)
    along = jnp.where(c == 0, z, x)

    def with_tail(k):
        own = lax.dynamic_slice_in_dim(block, KQ + (along + k) % 4 * 512, 512, 1)
        return jnp.concatenate([block[:, :KQ], own], axis=1)

    blocks = [with_tail(0)] + [crossed(with_tail(k), 0, k) for k in (1, 2, 3)]
    blocks, ffn_gain, ready = lax.optimization_barrier(
        (spread(place, blocks), ffn_gain, (down_weight, other_down))
    )
    lower_weights = load(*ready, "load_lower")
    ffn_gain = ffn_gain.reshape(1, D)
    gains = chunked(ffn_gain)
    blocks = [blocks[0]] + [crossed(blocks[k], 1, k) for k in (1, 2, 3)]
    blocks, gains, lower_weights = lax.optimization_barrier((blocks, gains, lower_weights))
    kept, *sent, tail = project(
        place, blocks, turned, near, (far, far_other)
    )
    taken = [around(sent[k - 1], k) for k in (1, 2, 3)]
    dispatched = mix(place, kept, taken, gains, tail)
    arrived = lax.all_to_all(dispatched, ("g", "z", "x", "y"), 0, 0, tiled=True)
    other = shift(arrived, "c")
    seen, squares, kept, sent, upper_weights = receive(
        place, arrived, gains, gate_weight.T, up_weight.T
    )
    taken = shift(sent, "c")
    sent, own = expert(place, seen, other, squares, gains, upper_weights)
    summed = lower(place, own, shift(sent, "c"), lower_weights, kept, taken, ffn_gain)
    returned = lax.all_to_all(summed, ("g", "z", "x", "y"), 0, 0, tiled=True)
    return combine(returned, parts)


def solution(mesh):
    fine = Mesh(mesh.devices.reshape(*SIZES.values()), ALL)
    rows = P(ALL, None)
    return jax.shard_map(
        per_device,
        mesh=fine,
        in_specs=(
            rows,
            rows,
            rows,
            rows,
            P(ALL, None, None),
            P(ALL, None, None),
            P(ALL),
            P(None, SECTION),
            P(),
            P(None, ALL),
            P(None, ALL),
            rows,
            rows,
            rows,
        ),
        out_specs=rows,
        check_vma=False,
    )
```

```python
import math

import jax
import jax.numpy as jnp
from jax import lax
from jax.experimental import pallas as pl
from jax.experimental.pallas import tpu as pltpu
from jax.sharding import Mesh, PartitionSpec as P

D = 7168
HEAD = 256
KALL = 16384
KHALF = KALL // 2
KQ = KHALF // 2
HID_DEV = 320
COLS = 112
EXPERTS = 8
BF = jnp.bfloat16
F32 = jnp.float32
SIZES = {"g": 2, "z": 4, "x": 4, "y": 2, "c": 2}
ALL = ("g", "z", "x", "y", "c")
SECTION = ("z", "x", "y", "c")


def shift(array, axis, step=1):
    n = SIZES[axis]
    return lax.ppermute(array, axis, [(i, (i + step) % n) for i in range(n)])


def others4(array, axis):
    return [shift(array, axis, 1), shift(array, axis, 2), shift(array, axis, 3)]


def ring_gy(array, step, swap=False):
    pairs = [
        (i * 2 + core, (i + step) % 4 * 2 + (1 - core if swap else core))
        for i in range(4)
        for core in range(2)
    ]
    return lax.ppermute(array, ("g", "y", "c"), pairs)


def around(array, k):
    return lax.ppermute(array, ("y", "c"), [(i, i ^ k) for i in range(4)])


def crossed(array, stage, step):
    pairs = []
    for z in range(4):
        for x in range(4):
            for c in range(2):
                along_z = c == stage
                to = ((z + step) % 4, x) if along_z else (z, (x + step) % 4)
                pairs.append(((z * 4 + x) * 2 + c, (to[0] * 4 + to[1]) * 2 + c))
    return lax.ppermute(array, ("z", "x", "c"), pairs)


def pair_ordered(own, other, mine):
    return jnp.where(
        mine == 0, jnp.stack([own, other]), jnp.stack([other, own])
    )


VMEM = pl.BlockSpec(memory_space=pltpu.VMEM)
SMEM = pl.BlockSpec(memory_space=pltpu.SMEM)
HBM = pl.BlockSpec(memory_space=pltpu.HBM)


def in_hbm(array):
    return pltpu.with_memory_space_constraint(array, pltpu.HBM)


def row_of(value, row):
    here = lax.broadcasted_iota(jnp.int32, value.shape, 0) == row
    return jnp.sum(jnp.where(here, value, 0.0), axis=0, keepdims=True)


def attend_kernel(
    lengths, routes, route_gates, place, q, hidden, k, v, new_key, new_value, turned,
    p0, p1, p2, p3, f0, h0, near, parts,
    keys, values, heads_of, flat, tails, sems,
):
    rows = q.shape[0]
    y, c = place[2], place[3]
    cuts = []
    for n, (of_c, of_y, part) in enumerate(((c, 1 - y, f0), (1 - c, 1 - y, h0), (1 - c, y, near))):
        at = pl.multiple_of(of_c * KHALF + of_y * KQ, KQ)
        cuts.append(pltpu.make_async_copy(
            turned.at[:, pl.ds(at, KQ)], part, sems.at[3, n]
        ))
    copies = [
        [
            pltpu.make_async_copy(source.at[r], kept.at[r], sems.at[i, r])
            for i, (source, kept) in enumerate(((k, keys), (v, values)))
        ]
        for r in range(rows)
    ]
    for copy in [copies[r][i] for p in range(0, rows, 2) for i in range(2) for r in (p, p + 1)]:
        copy.start()
    for copy in cuts:
        copy.start()
    scaling = 1.0 / math.sqrt(HEAD)
    scaled = q[...].astype(F32) * scaling
    for h in range(heads_of.shape[1]):
        heads_of[:, h, :] = scaled[:, h * HEAD : (h + 1) * HEAD]

    lane = lax.broadcasted_iota(jnp.int32, (1, 128), 1) - COLS
    line = lax.broadcasted_iota(jnp.int32, (rows, 128), 0)
    count = jnp.zeros((1, 128), F32)
    slots = jnp.zeros((rows, 128), F32)
    for r in range(rows):
        named = (lane == routes[r, 0]) | (lane == routes[r, 1]) | (lane == routes[r, 2])
        count = count + jnp.where(named, 1.0, 0.0)
        slots = slots + jnp.where((line == r) & named, count, 0.0)
    spot = lax.broadcasted_iota(jnp.int32, (1, 128), 1)
    half = lax.broadcasted_iota(jnp.int32, (2 * rows, 128), 0)
    of_expert, of_slot = spot // 16, spot % 2
    used = jnp.zeros((1, 128), jnp.int32)
    combined = jnp.zeros((2 * rows, 128), F32)
    for r in range(rows):
        gates = [jnp.full((1, 128), route_gates[r, k], jnp.int32).astype(F32) for k in range(3)]
        named = [of_expert == routes[r, k] for k in range(3)]
        chosen = jnp.zeros((1, 128), F32)
        for k in range(3):
            chosen = chosen + jnp.where(named[k], gates[k], 0.0)
        share = chosen / (gates[0] + gates[1] + gates[2])
        here = named[0] | named[1] | named[2]
        share = jnp.where(here & (used == of_slot), share, 0.0)
        used = used + jnp.where(here, 1, 0)
        high = share.astype(BF).astype(F32)
        combined = combined + jnp.where(half == r, high, 0.0)
        combined = combined + jnp.where(half == rows + r, share - high, 0.0)
    parts[...] = combined.astype(BF)
    stream = hidden[...].astype(F32)
    blank = jnp.zeros((rows, 128 - COLS), F32)
    for z in range(4):
        for x in range(4):
            for iy in range(2):
                for ic in range(2):
                    chunk = ((z * 4 + x) * 2 + iy) * 2 + ic
                    at = (x * 4 + z if ic else z * 4 + x) * 128
                    part = stream[:, chunk * COLS : (chunk + 1) * COLS]
                    part = jnp.concatenate([part, blank], axis=1) + slots
                    tails[ic * 2 + iy, :, at : at + 128] = part.astype(BF)

    own_keys, own_values = new_key[...].astype(F32), new_value[...].astype(F32)
    for pair in range(0, rows, 2):
        probs, own_probs = [], []
        for r in (pair, pair + 1):
            copies[r][0].wait()
        for r in (pair, pair + 1):
            queried = heads_of[r]
            itself = jnp.sum(queried * row_of(own_keys, r), axis=1, keepdims=True)
            cached = lax.dot_general(
                queried.astype(BF), keys[r], (((1,), (1,)), ((), ())),
                preferred_element_type=F32,
            )
            position = lax.broadcasted_iota(jnp.int32, cached.shape, 1)
            cached = jnp.where(position < lengths[r], cached, -jnp.inf)
            highest = jnp.maximum(jnp.max(cached, axis=1, keepdims=True), itself)
            cached_exp = jnp.exp(cached - highest)
            itself_exp = jnp.exp(itself - highest)
            share = 1.0 / (jnp.sum(cached_exp, axis=1, keepdims=True) + itself_exp)
            probs.append((cached_exp * share).astype(BF))
            own_probs.append((itself_exp * share).astype(BF).astype(F32))
        for r in (pair, pair + 1):
            copies[r][1].wait()
        for i, r in enumerate((pair, pair + 1)):
            mixture = jnp.dot(probs[i], values[r], preferred_element_type=F32)
            mixture = mixture + own_probs[i] * row_of(own_values, r)
            for h in range(mixture.shape[0]):
                at = h % 16 * HEAD
                flat[h // 16, r : r + 1, at : at + HEAD] = mixture[h : h + 1, :]
    for k, out in enumerate((p0, p1, p2, p3)):
        of_c = 1 - c if k % 2 else c
        of_y = 1 - y if k // 2 else y
        out[:, :KQ] = flat[of_c * 2 + of_y].astype(BF)
        out[:, KQ:] = tails[of_c * 2 + of_y]
    for copy in cuts:
        copy.wait()


def attend(
    queries, new_key, new_value, cache_keys, cache_values, lengths, routes, route_gates, hidden,
    place, turned,
):
    rows, context = cache_keys.shape[0], cache_keys.shape[1]
    heads = queries.shape[1] // HEAD
    return pl.pallas_call(
        attend_kernel,
        out_shape=(
            *(jax.ShapeDtypeStruct((rows, KQ + 16 * 128), BF),) * 4,
            jax.ShapeDtypeStruct((COLS, KQ), BF),
            jax.ShapeDtypeStruct((COLS, KQ), BF),
            jax.ShapeDtypeStruct((COLS, KQ), BF),
            jax.ShapeDtypeStruct((2 * rows, 128), BF),
        ),
        in_specs=[SMEM] * 4 + [VMEM] * 2 + [HBM] * 2 + [VMEM] * 2 + [HBM],
        out_specs=(VMEM,) * 8,
        scratch_shapes=[
            pltpu.VMEM((rows, context, HEAD), BF),
            pltpu.VMEM((rows, context, HEAD), BF),
            pltpu.VMEM((rows, heads, HEAD), F32),
            pltpu.VMEM((4, rows, KQ), F32),
            pltpu.VMEM((4, rows, 16 * 128), BF),
            pltpu.SemaphoreType.DMA((4, rows)),
        ],
        compiler_params=pltpu.CompilerParams(vmem_limit_bytes=24 << 20),
        cost_estimate=pl.CostEstimate(
            flops=4 * rows * heads * context * HEAD,
            bytes_accessed=4 * rows * context * HEAD,
            transcendentals=rows * heads * context,
        ),
        name="attend",
    )(
        in_hbm(lengths),
        in_hbm(routes),
        in_hbm(route_gates),
        place,
        in_hbm(queries),
        in_hbm(hidden),
        in_hbm(cache_keys),
        in_hbm(cache_values),
        in_hbm(new_key),
        in_hbm(new_value),
        in_hbm(turned),
    )


def at16(index):
    return pl.multiple_of(index, 16)


def spread_kernel(place, b0, b1, b2, b3, o0, o1, o2, o3):
    z, x, c = place[0], place[1], place[3]
    second = jnp.where(c == 0, x, z)
    for i, block in enumerate((b0, b1, b2, b3)):
        rows = slice(16 * i, 16 * i + 16)
        for k, out in enumerate((o0, o1, o2, o3)):
            out[rows, :KQ] = block[:, :KQ]
            lanes = pl.multiple_of(KQ + (second + k) % 4 * 128, 128)
            out[rows, KQ:] = block[:, pl.ds(lanes, 128)]


def spread(place, blocks):
    return pl.pallas_call(
        spread_kernel,
        out_shape=(jax.ShapeDtypeStruct((64, KQ + 128), BF),) * 4,
        in_specs=[SMEM] + [VMEM] * 4,
        out_specs=(VMEM,) * 4,
        compiler_params=pltpu.CompilerParams(vmem_limit_bytes=8 << 20),
        name="spread",
    )(place, *blocks)


def project_kernel(
    place, r0, r1, r2, r3, own, other, far, far_other, kept, s1, s2, s3, tail, w, rows, sems
):
    z, x, y, c = place[0], place[1], place[2], place[3]
    quarter = lambda start: pl.ds(pl.multiple_of(start, KQ), KQ)
    sources = (own.at[:, quarter(c * KHALF + y * KQ)], other, far, far_other)
    copies = [
        pltpu.make_async_copy(source, w.at[pl.ds(n * COLS, COLS), :], sems.at[n])
        for n, source in enumerate(sources)
    ]
    for copy in copies:
        copy.start()
    for k, block in enumerate((r0, r1, r2, r3)):
        for i in range(4):
            of_z = (z - jnp.where(c == 0, i, k) + 4) % 4
            of_x = (x - jnp.where(c == 0, k, i) + 4) % 4
            row = at16(of_z * 64 + of_x * 16)
            rows[pl.ds(row, 16), :] = block[16 * i : 16 * i + 16, :KQ]
            tail[pl.ds(row, 16), :] = block[16 * i : 16 * i + 16, KQ:]
    for copy in copies:
        copy.wait()
    product = lax.dot_general(
        w[...], rows[...], (((1,), (1,)), ((), ())), preferred_element_type=F32
    )
    kept[...] = product[:COLS]
    for i, sent in enumerate((s1, s2, s3)):
        sent[...] = product[(i + 1) * COLS : (i + 2) * COLS].astype(BF)


def project(place, blocks, own, other, fars):
    return pl.pallas_call(
        project_kernel,
        out_shape=(
            jax.ShapeDtypeStruct((COLS, 256), F32),
            *(jax.ShapeDtypeStruct((COLS, 256), BF),) * 3,
            jax.ShapeDtypeStruct((256, 128), BF),
        ),
        in_specs=[SMEM] + [VMEM] * 4 + [HBM] + [pl.BlockSpec(memory_space=pl.ANY)] * 3,
        out_specs=(VMEM,) * 5,
        scratch_shapes=[
            pltpu.VMEM((4 * COLS, KQ), BF),
            pltpu.VMEM((256, KQ), BF),
            pltpu.SemaphoreType.DMA((4,)),
        ],
        compiler_params=pltpu.CompilerParams(vmem_limit_bytes=12 << 20),
        name="project",
    )(place, *blocks, in_hbm(own), other, *fars)


def chunk_kernel(gain, out):
    for i in range(D // COLS):
        out[i : i + 1, :] = gain[:, i * COLS : (i + 1) * COLS]


def chunked(gain):
    return pl.pallas_call(
        chunk_kernel,
        out_shape=jax.ShapeDtypeStruct((D // COLS, COLS), F32),
        in_specs=[VMEM],
        out_specs=VMEM,
        compiler_params=pltpu.CompilerParams(vmem_limit_bytes=2 << 20),
        name="chunked",
    )(gain)


def mix_kernel(place, kept, r1, r2, r3, gains, tail, dispatched):
    chunk = ((place[0] * 4 + place[1]) * 2 + place[2]) * 2 + place[3]
    projected = kept[...] + r1[...].astype(F32) + (r2[...].astype(F32) + r3[...].astype(F32))
    back = tail[...].astype(F32).T[:COLS]
    widened = (back + projected).astype(BF).astype(F32)
    column = jnp.broadcast_to(row_of(gains[...], chunk), (8, COLS)).T[:, :1]
    carried = (widened * column).astype(BF)
    position = lax.broadcasted_iota(jnp.int32, (256, 128), 0)
    slot = lax.broadcasted_iota(jnp.int32, (256, 128), 1)
    z, x, y, c = position // 64, position // 16 % 4, position // 8 % 2, position // 4 % 2
    here = ((c * 4 + z) * 4 + x) * 2 + y == slot // 2
    rank = (slot % 2 + 1).astype(F32)
    ranks = tail[...].astype(F32)
    for e in range(EXPERTS):
        pick = jnp.where(here & (ranks[:, COLS + e : COLS + e + 1] == rank), 1.0, 0.0).astype(BF)
        block = jnp.dot(carried, pick, preferred_element_type=F32).astype(BF)
        for device in range(8):
            dispatched[8 * e + device] = block


def mix(place, kept, taken, gains, tail):
    return pl.pallas_call(
        mix_kernel,
        out_shape=jax.ShapeDtypeStruct((64, COLS, 128), BF),
        in_specs=[SMEM] + [VMEM] * 6,
        out_specs=VMEM,
        compiler_params=pltpu.CompilerParams(vmem_limit_bytes=12 << 20),
        name="mix",
    )(place, kept, *taken, gains, tail)


def load_kernel(first, second, out, sems):
    copies = []
    for i, source in enumerate((first, second)):
        for k in range(4):
            lanes = pl.ds(k * (D // 4), D // 4)
            copies.append(pltpu.make_async_copy(
                source.at[:, lanes], out.at[pl.ds(i * HID_DEV, HID_DEV), lanes], sems.at[i, k]
            ))
    for copy in copies:
        copy.start()
    for copy in copies:
        copy.wait()


def load(first, second, name):
    return pl.pallas_call(
        load_kernel,
        out_shape=jax.ShapeDtypeStruct((2 * HID_DEV, D), BF),
        in_specs=[HBM] * 2,
        out_specs=VMEM,
        scratch_shapes=[pltpu.SemaphoreType.DMA((2, 4))],
        compiler_params=pltpu.CompilerParams(vmem_limit_bytes=16 << 20),
        cost_estimate=pl.CostEstimate(
            flops=0, bytes_accessed=8 * HID_DEV * D, transcendentals=0
        ),
        name=name,
    )(in_hbm(first), in_hbm(second))


def squares_of(block, scales, chunk_of_c):
    i, c = chunk_of_c
    scale = jnp.where(c == 0, scales[:, 2 * i : 2 * i + 1], scales[:, 2 * i + 1 : 2 * i + 2])
    value = block.astype(F32) * scale
    return jnp.sum((value * value).reshape(14, 8, 128), axis=0)


def receive_kernel(
    place, arrived, gains, gate, up, columns, squares, kept, sent, weights, sems
):
    x, y, c = place[1], place[2], place[3]
    copies = []
    for i, source in enumerate((gate, up)):
        for k in range(4):
            lanes = pl.ds(k * (D // 4), D // 4)
            copies.append(pltpu.make_async_copy(
                source.at[:, lanes], weights.at[pl.ds(i * HID_DEV, HID_DEV), lanes], sems.at[i, k]
            ))
    for copy in copies:
        copy.start()
    scales = 1.0 / gains[...].T
    for g in range(2):
        total = jnp.zeros((8, 128), F32)
        lanes = slice(128 * g, 128 * g + 128)
        for i in range(32):
            block = arrived[32 * g + i]
            columns[pl.ds(at16((2 * i + c) * COLS), COLS), lanes] = block
            columns[pl.ds(at16((2 * i + 1 - c) * COLS), COLS), lanes] = jnp.zeros_like(block)
            total = total + squares_of(block, scales, (i, c))
        squares[:, lanes] = total
    row = lax.broadcasted_iota(jnp.int32, (32, 256), 0)
    lane = lax.broadcasted_iota(jnp.int32, (32, 256), 1)
    of_c = jnp.where(row < 16, c, 1 - c)
    slot = ((of_c * 4 + row // 2 % 4) * 4 + x) * 2 + y
    mine = lane == row // 8 % 2 * 128 + slot * 2 + row % 2
    residual = lax.dot_general(
        jnp.where(mine, 1.0, 0.0).astype(BF), columns[...],
        (((1,), (1,)), ((), ())), preferred_element_type=F32,
    ).astype(BF)
    kept[...] = residual[:16]
    sent[...] = residual[16:]
    for copy in copies:
        copy.wait()


def receive(place, arrived, gains, gate, up):
    return pl.pallas_call(
        receive_kernel,
        out_shape=(
            jax.ShapeDtypeStruct((D, 256), BF),
            jax.ShapeDtypeStruct((8, 256), F32),
            jax.ShapeDtypeStruct((16, D), BF),
            jax.ShapeDtypeStruct((16, D), BF),
            jax.ShapeDtypeStruct((2 * HID_DEV, D), BF),
        ),
        in_specs=[SMEM] + [VMEM] * 2 + [HBM] * 2,
        out_specs=(VMEM,) * 5,
        scratch_shapes=[pltpu.SemaphoreType.DMA((2, 4))],
        compiler_params=pltpu.CompilerParams(vmem_limit_bytes=16 << 20),
        name="receive",
    )(place, arrived, gains, in_hbm(gate), in_hbm(up))


def expert_kernel(place, seen, other, own_squares, gains, weights, sent, kept, columns, act):
    c = place[3]
    scales = 1.0 / gains[...].T
    other_squares = [jnp.zeros((8, 128), F32)] * 2
    for i in range(32):
        own_rows = pl.ds(at16((2 * i + c) * COLS), COLS)
        other_rows = pl.ds(at16((2 * i + 1 - c) * COLS), COLS)
        columns[own_rows, :] = seen[own_rows, :]
        for g in range(2):
            block = other[32 * g + i]
            columns[other_rows, 128 * g : 128 * g + 128] = block
            other_squares[g] = other_squares[g] + squares_of(block, scales, (i, 1 - c))
    product = jnp.dot(weights[...], columns[...], preferred_element_type=F32)
    squares = own_squares[...] + jnp.concatenate(other_squares, axis=1)
    scale = lax.rsqrt(jnp.sum(squares, axis=0, keepdims=True) / D + 1e-05)
    gated = product[:HID_DEV] * scale
    upward = product[HID_DEV:] * scale
    activated = gated / (1.0 + jnp.exp(-gated)) * upward
    act[...] = activated.T.astype(BF)
    for g in range(2):
        sent[g * 64 : g * 64 + 64, :] = act[pl.ds(at16(g * 128 + (1 - c) * 64), 64), :]
        kept[g * 64 : g * 64 + 64, :] = act[pl.ds(at16(g * 128 + c * 64), 64), :]


def expert(place, seen, other, own_squares, gains, weights):
    return pl.pallas_call(
        expert_kernel,
        out_shape=(jax.ShapeDtypeStruct((128, HID_DEV), BF),) * 2,
        in_specs=[SMEM] + [VMEM] * 5,
        out_specs=(VMEM,) * 2,
        scratch_shapes=[pltpu.VMEM((D, 256), BF), pltpu.VMEM((256, HID_DEV), BF)],
        compiler_params=pltpu.CompilerParams(vmem_limit_bytes=16 << 20),
        name="expert",
    )(place, seen, other, own_squares, gains, weights)


def lower_kernel(place, own, other, weights, kept, taken, gain, out, act):
    x, y = place[1], place[2]
    act[:, :HID_DEV] = own[...]
    act[:, HID_DEV:] = other[...]
    row = lax.broadcasted_iota(jnp.int32, (128, 16), 0)
    column = lax.broadcasted_iota(jnp.int32, (128, 16), 1)
    here = (row // 2 % 8 == x * 2 + y) & (row // 16 * 2 + row % 2 == column)
    place_in = jnp.where(here, 1.0, 0.0).astype(BF)
    width = D // 4
    for k in range(4):
        lanes = slice(k * width, (k + 1) * width)
        part = jnp.dot(act[...], weights[:, lanes], preferred_element_type=F32)
        residual = (kept[:, lanes] + taken[:, lanes]).astype(F32) / gain[:, lanes]
        high = residual.astype(BF)
        low = (residual - high.astype(F32)).astype(BF)
        part = part + jnp.dot(place_in, high, preferred_element_type=F32)
        part = part + jnp.dot(place_in, low, preferred_element_type=F32)
        out[:, :, lanes] = part.astype(BF).reshape(64, 2, width)


def lower(place, own, other, weights, kept, taken, gain):
    return pl.pallas_call(
        lower_kernel,
        out_shape=jax.ShapeDtypeStruct((64, 2, D), BF),
        in_specs=[SMEM] + [VMEM] * 6,
        out_specs=VMEM,
        scratch_shapes=[pltpu.VMEM((128, 2 * HID_DEV), BF)],
        compiler_params=pltpu.CompilerParams(vmem_limit_bytes=16 << 20),
        name="lower",
    )(place, own, other, weights, kept, taken, gain)


def combine_kernel(returned, weights, out):
    rows = out.shape[0]
    width = D // 4
    for k in range(4):
        lanes = slice(k * width, (k + 1) * width)
        sums = returned[:, :, lanes].reshape(128, width)
        total = jnp.dot(weights[...], sums, preferred_element_type=F32)
        out[:, lanes] = (total[:rows] + total[rows:]).astype(BF)


def combine(returned, weights):
    return pl.pallas_call(
        combine_kernel,
        out_shape=jax.ShapeDtypeStruct((weights.shape[0] // 2, D), BF),
        in_specs=[VMEM] * 2,
        out_specs=VMEM,
        compiler_params=pltpu.CompilerParams(vmem_limit_bytes=8 << 20),
        name="combine",
    )(returned, weights)


def per_device(
    hidden,
    queries,
    new_key,
    new_value,
    cache_keys,
    cache_values,
    lengths,
    out_weight,
    ffn_gain,
    gate_weight,
    up_weight,
    down_weight,
    routes,
    route_gates,
):
    z, x, y, c = (lax.axis_index(a) for a in SECTION)
    chunk = ((z * 4 + x) * 2 + y) * 2 + c
    place = jnp.stack([z, x, y, c]).astype(jnp.int32)

    turned = out_weight.T

    other_down = shift(down_weight, "c")
    *payloads, f0, h0, near, parts = attend(
        queries, new_key, new_value, cache_keys, cache_values, lengths, routes, route_gates,
        hidden, place, turned,
    )
    near = shift(near, "c")
    far, far_other, near, other_down = lax.optimization_barrier((f0, h0, near, other_down))
    far, far_other = ring_gy(far, 1), ring_gy(far_other, -1, True)
    got = [payloads[0]] + [around(payloads[k], k) for k in (1, 2, 3)]
    block = pair_ordered(pair_ordered(got[0], got[1], c), pair_ordered(got[2], got[3], c), y)
    block = block.reshape(16, KQ + 2048)
    along = jnp.where(c == 0, z, x)

    def with_tail(k):
        own = lax.dynamic_slice_in_dim(block, KQ + (along + k) % 4 * 512, 512, 1)
        return jnp.concatenate([block[:, :KQ], own], axis=1)

    blocks = [with_tail(0)] + [crossed(with_tail(k), 0, k) for k in (1, 2, 3)]
    blocks, ffn_gain, ready = lax.optimization_barrier(
        (spread(place, blocks), ffn_gain, (down_weight, other_down))
    )
    lower_weights = load(*ready, "load_lower")
    ffn_gain = ffn_gain.reshape(1, D)
    gains = chunked(ffn_gain)
    blocks = [blocks[0]] + [crossed(blocks[k], 1, k) for k in (1, 2, 3)]
    blocks, gains, lower_weights = lax.optimization_barrier((blocks, gains, lower_weights))
    kept, *sent, tail = project(
        place, blocks, turned, near, (far, far_other)
    )
    taken = [around(sent[k - 1], k) for k in (1, 2, 3)]
    dispatched = mix(place, kept, taken, gains, tail)
    arrived = lax.all_to_all(dispatched, ("g", "z", "x", "y"), 0, 0, tiled=True)
    other = shift(arrived, "c")
    seen, squares, kept, sent, upper_weights = receive(
        place, arrived, gains, gate_weight.T, up_weight.T
    )
    taken = shift(sent, "c")
    sent, own = expert(place, seen, other, squares, gains, upper_weights)
    summed = lower(place, own, shift(sent, "c"), lower_weights, kept, taken, ffn_gain)
    returned = lax.all_to_all(summed, ("g", "z", "x", "y"), 0, 0, tiled=True)
    return combine(returned, parts)


def solution(mesh):
    fine = Mesh(mesh.devices.reshape(*SIZES.values()), ALL)
    rows = P(ALL, None)
    return jax.shard_map(
        per_device,
        mesh=fine,
        in_specs=(
            rows,
            rows,
            rows,
            rows,
            P(ALL, None, None),
            P(ALL, None, None),
            P(ALL),
            P(None, SECTION),
            P(),
            P(None, ALL),
            P(None, ALL),
            rows,
            rows,
            rows,
        ),
        out_specs=rows,
        check_vma=False,
    )
```

```python
import math

import jax
import jax.numpy as jnp
from jax import lax
from jax.experimental import pallas as pl
from jax.experimental.pallas import tpu as pltpu
from jax.sharding import Mesh, PartitionSpec as P

D = 7168
HEAD = 256
KALL = 16384
KHALF = KALL // 2
KQ = KHALF // 2
HID_DEV = 320
COLS = 112
EXPERTS = 8
BF = jnp.bfloat16
F32 = jnp.float32
SIZES = {"g": 2, "z": 4, "x": 4, "y": 2, "c": 2}
ALL = ("g", "z", "x", "y", "c")
SECTION = ("z", "x", "y", "c")


def shift(array, axis, step=1):
    n = SIZES[axis]
    return lax.ppermute(array, axis, [(i, (i + step) % n) for i in range(n)])


def others4(array, axis):
    return [shift(array, axis, 1), shift(array, axis, 2), shift(array, axis, 3)]


def ring_gy(array, step, swap=False):
    pairs = [
        (i * 2 + core, (i + step) % 4 * 2 + (1 - core if swap else core))
        for i in range(4)
        for core in range(2)
    ]
    return lax.ppermute(array, ("g", "y", "c"), pairs)


def around(array, k):
    return lax.ppermute(array, ("y", "c"), [(i, i ^ k) for i in range(4)])


def crossed(array, stage, step):
    pairs = []
    for z in range(4):
        for x in range(4):
            for c in range(2):
                along_z = c == stage
                to = ((z + step) % 4, x) if along_z else (z, (x + step) % 4)
                pairs.append(((z * 4 + x) * 2 + c, (to[0] * 4 + to[1]) * 2 + c))
    return lax.ppermute(array, ("z", "x", "c"), pairs)


def pair_ordered(own, other, mine):
    return jnp.where(
        mine == 0, jnp.stack([own, other]), jnp.stack([other, own])
    )


VMEM = pl.BlockSpec(memory_space=pltpu.VMEM)
SMEM = pl.BlockSpec(memory_space=pltpu.SMEM)
HBM = pl.BlockSpec(memory_space=pltpu.HBM)


def in_hbm(array):
    return pltpu.with_memory_space_constraint(array, pltpu.HBM)


def row_of(value, row):
    here = lax.broadcasted_iota(jnp.int32, value.shape, 0) == row
    return jnp.sum(jnp.where(here, value, 0.0), axis=0, keepdims=True)


def attend_kernel(
    lengths, routes, route_gates, place, q, hidden, k, v, new_key, new_value, turned,
    p0, p1, p2, p3, f0, h0, near, parts,
    keys, values, heads_of, flat, tails, sems,
):
    rows = q.shape[0]
    y, c = place[2], place[3]
    cuts = []
    for n, (of_c, of_y, part) in enumerate(((c, 1 - y, f0), (1 - c, 1 - y, h0), (1 - c, y, near))):
        at = pl.multiple_of(of_c * KHALF + of_y * KQ, KQ)
        cuts.append(pltpu.make_async_copy(
            turned.at[:, pl.ds(at, KQ)], part, sems.at[3, n]
        ))
    copies = [
        [
            pltpu.make_async_copy(source.at[r], kept.at[r], sems.at[i, r])
            for i, (source, kept) in enumerate(((k, keys), (v, values)))
        ]
        for r in range(rows)
    ]
    for copy in [copies[r][i] for p in range(0, rows, 2) for i in range(2) for r in (p, p + 1)]:
        copy.start()
    for copy in cuts:
        copy.start()
    scaling = 1.0 / math.sqrt(HEAD)
    scaled = q[...].astype(F32) * scaling
    for h in range(heads_of.shape[1]):
        heads_of[:, h, :] = scaled[:, h * HEAD : (h + 1) * HEAD]

    lane = lax.broadcasted_iota(jnp.int32, (1, 128), 1) - COLS
    line = lax.broadcasted_iota(jnp.int32, (rows, 128), 0)
    count = jnp.zeros((1, 128), F32)
    slots = jnp.zeros((rows, 128), F32)
    for r in range(rows):
        named = (lane == routes[r, 0]) | (lane == routes[r, 1]) | (lane == routes[r, 2])
        count = count + jnp.where(named, 1.0, 0.0)
        slots = slots + jnp.where((line == r) & named, count, 0.0)
    spot = lax.broadcasted_iota(jnp.int32, (1, 128), 1)
    half = lax.broadcasted_iota(jnp.int32, (2 * rows, 128), 0)
    of_expert, of_slot = spot // 16, spot % 2
    used = jnp.zeros((1, 128), jnp.int32)
    combined = jnp.zeros((2 * rows, 128), F32)
    for r in range(rows):
        gates = [jnp.full((1, 128), route_gates[r, k], jnp.int32).astype(F32) for k in range(3)]
        named = [of_expert == routes[r, k] for k in range(3)]
        chosen = jnp.zeros((1, 128), F32)
        for k in range(3):
            chosen = chosen + jnp.where(named[k], gates[k], 0.0)
        share = chosen / (gates[0] + gates[1] + gates[2])
        here = named[0] | named[1] | named[2]
        share = jnp.where(here & (used == of_slot), share, 0.0)
        used = used + jnp.where(here, 1, 0)
        high = share.astype(BF).astype(F32)
        combined = combined + jnp.where(half == r, high, 0.0)
        combined = combined + jnp.where(half == rows + r, share - high, 0.0)
    parts[...] = combined.astype(BF)
    stream = hidden[...].astype(F32)
    blank = jnp.zeros((rows, 128 - COLS), F32)
    for z in range(4):
        for x in range(4):
            for iy in range(2):
                for ic in range(2):
                    chunk = ((z * 4 + x) * 2 + iy) * 2 + ic
                    at = (x * 4 + z if ic else z * 4 + x) * 128
                    part = stream[:, chunk * COLS : (chunk + 1) * COLS]
                    part = jnp.concatenate([part, blank], axis=1) + slots
                    tails[ic * 2 + iy, :, at : at + 128] = part.astype(BF)

    own_keys, own_values = new_key[...].astype(F32), new_value[...].astype(F32)
    for pair in range(0, rows, 2):
        probs, own_probs = [], []
        for r in (pair, pair + 1):
            copies[r][0].wait()
        for r in (pair, pair + 1):
            queried = heads_of[r]
            itself = jnp.sum(queried * row_of(own_keys, r), axis=1, keepdims=True)
            cached = lax.dot_general(
                queried.astype(BF), keys[r], (((1,), (1,)), ((), ())),
                preferred_element_type=F32,
            )
            position = lax.broadcasted_iota(jnp.int32, cached.shape, 1)
            cached = jnp.where(position < lengths[r], cached, -jnp.inf)
            highest = jnp.maximum(jnp.max(cached, axis=1, keepdims=True), itself)
            cached_exp = jnp.exp(cached - highest)
            itself_exp = jnp.exp(itself - highest)
            share = 1.0 / (jnp.sum(cached_exp, axis=1, keepdims=True) + itself_exp)
            probs.append((cached_exp * share).astype(BF))
            own_probs.append((itself_exp * share).astype(BF).astype(F32))
        for r in (pair, pair + 1):
            copies[r][1].wait()
        for i, r in enumerate((pair, pair + 1)):
            mixture = jnp.dot(probs[i], values[r], preferred_element_type=F32)
            mixture = mixture + own_probs[i] * row_of(own_values, r)
            for h in range(mixture.shape[0]):
                at = h % 16 * HEAD
                flat[h // 16, r : r + 1, at : at + HEAD] = mixture[h : h + 1, :]
    for k, out in enumerate((p0, p1, p2, p3)):
        of_c = 1 - c if k % 2 else c
        of_y = 1 - y if k // 2 else y
        out[:, :KQ] = flat[of_c * 2 + of_y].astype(BF)
        out[:, KQ:] = tails[of_c * 2 + of_y]
    for copy in cuts:
        copy.wait()


def attend(
    queries, new_key, new_value, cache_keys, cache_values, lengths, routes, route_gates, hidden,
    place, turned,
):
    rows, context = cache_keys.shape[0], cache_keys.shape[1]
    heads = queries.shape[1] // HEAD
    return pl.pallas_call(
        attend_kernel,
        out_shape=(
            *(jax.ShapeDtypeStruct((rows, KQ + 16 * 128), BF),) * 4,
            jax.ShapeDtypeStruct((COLS, KQ), BF),
            jax.ShapeDtypeStruct((COLS, KQ), BF),
            jax.ShapeDtypeStruct((COLS, KQ), BF),
            jax.ShapeDtypeStruct((2 * rows, 128), BF),
        ),
        in_specs=[SMEM] * 4 + [VMEM] * 2 + [HBM] * 2 + [VMEM] * 2 + [HBM],
        out_specs=(VMEM,) * 8,
        scratch_shapes=[
            pltpu.VMEM((rows, context, HEAD), BF),
            pltpu.VMEM((rows, context, HEAD), BF),
            pltpu.VMEM((rows, heads, HEAD), F32),
            pltpu.VMEM((4, rows, KQ), F32),
            pltpu.VMEM((4, rows, 16 * 128), BF),
            pltpu.SemaphoreType.DMA((4, rows)),
        ],
        compiler_params=pltpu.CompilerParams(vmem_limit_bytes=24 << 20),
        cost_estimate=pl.CostEstimate(
            flops=4 * rows * heads * context * HEAD,
            bytes_accessed=4 * rows * context * HEAD,
            transcendentals=rows * heads * context,
        ),
        name="attend",
    )(
        in_hbm(lengths),
        in_hbm(routes),
        in_hbm(route_gates),
        place,
        in_hbm(queries),
        in_hbm(hidden),
        in_hbm(cache_keys),
        in_hbm(cache_values),
        in_hbm(new_key),
        in_hbm(new_value),
        in_hbm(turned),
    )


def at16(index):
    return pl.multiple_of(index, 16)


def spread_kernel(place, b0, b1, b2, b3, o0, o1, o2, o3):
    z, x, c = place[0], place[1], place[3]
    second = jnp.where(c == 0, x, z)
    for i, block in enumerate((b0, b1, b2, b3)):
        rows = slice(16 * i, 16 * i + 16)
        for k, out in enumerate((o0, o1, o2, o3)):
            out[rows, :KQ] = block[:, :KQ]
            lanes = pl.multiple_of(KQ + (second + k) % 4 * 128, 128)
            out[rows, KQ:] = block[:, pl.ds(lanes, 128)]


def spread(place, blocks):
    return pl.pallas_call(
        spread_kernel,
        out_shape=(jax.ShapeDtypeStruct((64, KQ + 128), BF),) * 4,
        in_specs=[SMEM] + [VMEM] * 4,
        out_specs=(VMEM,) * 4,
        compiler_params=pltpu.CompilerParams(vmem_limit_bytes=8 << 20),
        name="spread",
    )(place, *blocks)


def own_kernel(place, turned, out, sem):
    y, c = place[2], place[3]
    quarter = pl.ds(pl.multiple_of(c * KHALF + y * KQ, KQ), KQ)
    copy = pltpu.make_async_copy(turned.at[:, quarter], out, sem.at[0])
    copy.start()
    copy.wait()


def own_quarter(place, turned):
    return pl.pallas_call(
        own_kernel,
        out_shape=jax.ShapeDtypeStruct((COLS, KQ), BF),
        in_specs=[SMEM, HBM],
        out_specs=VMEM,
        scratch_shapes=[pltpu.SemaphoreType.DMA((1,))],
        compiler_params=pltpu.CompilerParams(vmem_limit_bytes=4 << 20),
        name="own_quarter",
    )(place, in_hbm(turned))


def project_kernel(
    place, r0, r1, r2, r3, own, other, far, far_other, kept, s1, s2, s3, tail, rows
):
    z, x, c = place[0], place[1], place[3]
    for k, block in enumerate((r0, r1, r2, r3)):
        for i in range(4):
            of_z = (z - jnp.where(c == 0, i, k) + 4) % 4
            of_x = (x - jnp.where(c == 0, k, i) + 4) % 4
            row = at16(of_z * 64 + of_x * 16)
            rows[pl.ds(row, 16), :] = block[16 * i : 16 * i + 16, :KQ]
            tail[pl.ds(row, 16), :] = block[16 * i : 16 * i + 16, KQ:]
    weights = jnp.concatenate([own[...], other[...], far[...], far_other[...]], axis=0)
    product = lax.dot_general(
        weights, rows[...], (((1,), (1,)), ((), ())), preferred_element_type=F32
    )
    kept[...] = product[:COLS]
    for i, sent in enumerate((s1, s2, s3)):
        sent[...] = product[(i + 1) * COLS : (i + 2) * COLS].astype(BF)


def project(place, blocks, own, other, fars):
    return pl.pallas_call(
        project_kernel,
        out_shape=(
            jax.ShapeDtypeStruct((COLS, 256), F32),
            *(jax.ShapeDtypeStruct((COLS, 256), BF),) * 3,
            jax.ShapeDtypeStruct((256, 128), BF),
        ),
        in_specs=[SMEM] + [VMEM] * 8,
        out_specs=(VMEM,) * 5,
        scratch_shapes=[
            pltpu.VMEM((256, KQ), BF),
        ],
        compiler_params=pltpu.CompilerParams(vmem_limit_bytes=12 << 20),
        name="project",
    )(place, *blocks, own, other, *fars)


def chunk_kernel(gain, out):
    for i in range(D // COLS):
        out[i : i + 1, :] = gain[:, i * COLS : (i + 1) * COLS]


def chunked(gain):
    return pl.pallas_call(
        chunk_kernel,
        out_shape=jax.ShapeDtypeStruct((D // COLS, COLS), F32),
        in_specs=[VMEM],
        out_specs=VMEM,
        compiler_params=pltpu.CompilerParams(vmem_limit_bytes=2 << 20),
        name="chunked",
    )(gain)


def mix_kernel(place, kept, r1, r2, r3, gains, tail, dispatched):
    chunk = ((place[0] * 4 + place[1]) * 2 + place[2]) * 2 + place[3]
    projected = kept[...] + r1[...].astype(F32) + (r2[...].astype(F32) + r3[...].astype(F32))
    back = tail[...].astype(F32).T[:COLS]
    widened = (back + projected).astype(BF).astype(F32)
    column = jnp.broadcast_to(row_of(gains[...], chunk), (8, COLS)).T[:, :1]
    carried = (widened * column).astype(BF)
    position = lax.broadcasted_iota(jnp.int32, (256, 128), 0)
    slot = lax.broadcasted_iota(jnp.int32, (256, 128), 1)
    z, x, y, c = position // 64, position // 16 % 4, position // 8 % 2, position // 4 % 2
    here = ((c * 4 + z) * 4 + x) * 2 + y == slot // 2
    rank = (slot % 2 + 1).astype(F32)
    ranks = tail[...].astype(F32)
    for e in range(EXPERTS):
        pick = jnp.where(here & (ranks[:, COLS + e : COLS + e + 1] == rank), 1.0, 0.0).astype(BF)
        block = jnp.dot(carried, pick, preferred_element_type=F32).astype(BF)
        for device in range(8):
            dispatched[8 * e + device] = block


def mix(place, kept, taken, gains, tail):
    return pl.pallas_call(
        mix_kernel,
        out_shape=jax.ShapeDtypeStruct((64, COLS, 128), BF),
        in_specs=[SMEM] + [VMEM] * 6,
        out_specs=VMEM,
        compiler_params=pltpu.CompilerParams(vmem_limit_bytes=12 << 20),
        name="mix",
    )(place, kept, *taken, gains, tail)


def load_kernel(first, second, out, sems):
    copies = []
    for i, source in enumerate((first, second)):
        for k in range(4):
            lanes = pl.ds(k * (D // 4), D // 4)
            copies.append(pltpu.make_async_copy(
                source.at[:, lanes], out.at[pl.ds(i * HID_DEV, HID_DEV), lanes], sems.at[i, k]
            ))
    for copy in copies:
        copy.start()
    for copy in copies:
        copy.wait()


def load(first, second, name):
    return pl.pallas_call(
        load_kernel,
        out_shape=jax.ShapeDtypeStruct((2 * HID_DEV, D), BF),
        in_specs=[HBM] * 2,
        out_specs=VMEM,
        scratch_shapes=[pltpu.SemaphoreType.DMA((2, 4))],
        compiler_params=pltpu.CompilerParams(vmem_limit_bytes=16 << 20),
        cost_estimate=pl.CostEstimate(
            flops=0, bytes_accessed=8 * HID_DEV * D, transcendentals=0
        ),
        name=name,
    )(in_hbm(first), in_hbm(second))


def squares_of(block, scales, chunk_of_c):
    i, c = chunk_of_c
    scale = jnp.where(c == 0, scales[:, 2 * i : 2 * i + 1], scales[:, 2 * i + 1 : 2 * i + 2])
    value = block.astype(F32) * scale
    return jnp.sum((value * value).reshape(14, 8, 128), axis=0)


def receive_kernel(
    place, arrived, gains, gate, up, columns, squares, kept, sent, weights, sems
):
    x, y, c = place[1], place[2], place[3]
    copies = []
    for i, source in enumerate((gate, up)):
        for k in range(4):
            lanes = pl.ds(k * (D // 4), D // 4)
            copies.append(pltpu.make_async_copy(
                source.at[:, lanes], weights.at[pl.ds(i * HID_DEV, HID_DEV), lanes], sems.at[i, k]
            ))
    for copy in copies:
        copy.start()
    scales = 1.0 / gains[...].T
    for g in range(2):
        total = jnp.zeros((8, 128), F32)
        lanes = slice(128 * g, 128 * g + 128)
        for i in range(32):
            block = arrived[32 * g + i]
            columns[pl.ds(at16((2 * i + c) * COLS), COLS), lanes] = block
            columns[pl.ds(at16((2 * i + 1 - c) * COLS), COLS), lanes] = jnp.zeros_like(block)
            total = total + squares_of(block, scales, (i, c))
        squares[:, lanes] = total
    row = lax.broadcasted_iota(jnp.int32, (32, 256), 0)
    lane = lax.broadcasted_iota(jnp.int32, (32, 256), 1)
    of_c = jnp.where(row < 16, c, 1 - c)
    slot = ((of_c * 4 + row // 2 % 4) * 4 + x) * 2 + y
    mine = lane == row // 8 % 2 * 128 + slot * 2 + row % 2
    residual = lax.dot_general(
        jnp.where(mine, 1.0, 0.0).astype(BF), columns[...],
        (((1,), (1,)), ((), ())), preferred_element_type=F32,
    ).astype(BF)
    kept[...] = residual[:16]
    sent[...] = residual[16:]
    for copy in copies:
        copy.wait()


def receive(place, arrived, gains, gate, up):
    return pl.pallas_call(
        receive_kernel,
        out_shape=(
            jax.ShapeDtypeStruct((D, 256), BF),
            jax.ShapeDtypeStruct((8, 256), F32),
            jax.ShapeDtypeStruct((16, D), BF),
            jax.ShapeDtypeStruct((16, D), BF),
            jax.ShapeDtypeStruct((2 * HID_DEV, D), BF),
        ),
        in_specs=[SMEM] + [VMEM] * 2 + [HBM] * 2,
        out_specs=(VMEM,) * 5,
        scratch_shapes=[pltpu.SemaphoreType.DMA((2, 4))],
        compiler_params=pltpu.CompilerParams(vmem_limit_bytes=16 << 20),
        name="receive",
    )(place, arrived, gains, in_hbm(gate), in_hbm(up))


def expert_kernel(place, seen, other, own_squares, gains, weights, sent, kept, columns, act):
    c = place[3]
    scales = 1.0 / gains[...].T
    other_squares = [jnp.zeros((8, 128), F32)] * 2
    for i in range(32):
        own_rows = pl.ds(at16((2 * i + c) * COLS), COLS)
        other_rows = pl.ds(at16((2 * i + 1 - c) * COLS), COLS)
        columns[own_rows, :] = seen[own_rows, :]
        for g in range(2):
            block = other[32 * g + i]
            columns[other_rows, 128 * g : 128 * g + 128] = block
            other_squares[g] = other_squares[g] + squares_of(block, scales, (i, 1 - c))
    product = jnp.dot(weights[...], columns[...], preferred_element_type=F32)
    squares = own_squares[...] + jnp.concatenate(other_squares, axis=1)
    scale = lax.rsqrt(jnp.sum(squares, axis=0, keepdims=True) / D + 1e-05)
    gated = product[:HID_DEV] * scale
    upward = product[HID_DEV:] * scale
    activated = gated / (1.0 + jnp.exp(-gated)) * upward
    act[...] = activated.T.astype(BF)
    for g in range(2):
        sent[g * 64 : g * 64 + 64, :] = act[pl.ds(at16(g * 128 + (1 - c) * 64), 64), :]
        kept[g * 64 : g * 64 + 64, :] = act[pl.ds(at16(g * 128 + c * 64), 64), :]


def expert(place, seen, other, own_squares, gains, weights):
    return pl.pallas_call(
        expert_kernel,
        out_shape=(jax.ShapeDtypeStruct((128, HID_DEV), BF),) * 2,
        in_specs=[SMEM] + [VMEM] * 5,
        out_specs=(VMEM,) * 2,
        scratch_shapes=[pltpu.VMEM((D, 256), BF), pltpu.VMEM((256, HID_DEV), BF)],
        compiler_params=pltpu.CompilerParams(vmem_limit_bytes=16 << 20),
        name="expert",
    )(place, seen, other, own_squares, gains, weights)


def lower_kernel(place, own, other, weights, kept, taken, gain, out, act):
    x, y = place[1], place[2]
    act[:, :HID_DEV] = own[...]
    act[:, HID_DEV:] = other[...]
    row = lax.broadcasted_iota(jnp.int32, (128, 16), 0)
    column = lax.broadcasted_iota(jnp.int32, (128, 16), 1)
    here = (row // 2 % 8 == x * 2 + y) & (row // 16 * 2 + row % 2 == column)
    place_in = jnp.where(here, 1.0, 0.0).astype(BF)
    width = D // 4
    for k in range(4):
        lanes = slice(k * width, (k + 1) * width)
        part = jnp.dot(act[...], weights[:, lanes], preferred_element_type=F32)
        residual = (kept[:, lanes] + taken[:, lanes]).astype(F32) / gain[:, lanes]
        high = residual.astype(BF)
        low = (residual - high.astype(F32)).astype(BF)
        part = part + jnp.dot(place_in, high, preferred_element_type=F32)
        part = part + jnp.dot(place_in, low, preferred_element_type=F32)
        out[:, :, lanes] = part.astype(BF).reshape(64, 2, width)


def lower(place, own, other, weights, kept, taken, gain):
    return pl.pallas_call(
        lower_kernel,
        out_shape=jax.ShapeDtypeStruct((64, 2, D), BF),
        in_specs=[SMEM] + [VMEM] * 6,
        out_specs=VMEM,
        scratch_shapes=[pltpu.VMEM((128, 2 * HID_DEV), BF)],
        compiler_params=pltpu.CompilerParams(vmem_limit_bytes=16 << 20),
        name="lower",
    )(place, own, other, weights, kept, taken, gain)


def combine_kernel(returned, weights, out):
    rows = out.shape[0]
    width = D // 4
    for k in range(4):
        lanes = slice(k * width, (k + 1) * width)
        sums = returned[:, :, lanes].reshape(128, width)
        total = jnp.dot(weights[...], sums, preferred_element_type=F32)
        out[:, lanes] = (total[:rows] + total[rows:]).astype(BF)


def combine(returned, weights):
    return pl.pallas_call(
        combine_kernel,
        out_shape=jax.ShapeDtypeStruct((weights.shape[0] // 2, D), BF),
        in_specs=[VMEM] * 2,
        out_specs=VMEM,
        compiler_params=pltpu.CompilerParams(vmem_limit_bytes=8 << 20),
        name="combine",
    )(returned, weights)


def per_device(
    hidden,
    queries,
    new_key,
    new_value,
    cache_keys,
    cache_values,
    lengths,
    out_weight,
    ffn_gain,
    gate_weight,
    up_weight,
    down_weight,
    routes,
    route_gates,
):
    z, x, y, c = (lax.axis_index(a) for a in SECTION)
    chunk = ((z * 4 + x) * 2 + y) * 2 + c
    place = jnp.stack([z, x, y, c]).astype(jnp.int32)

    turned = out_weight.T

    other_down = shift(down_weight, "c")
    *payloads, f0, h0, near, parts = attend(
        queries, new_key, new_value, cache_keys, cache_values, lengths, routes, route_gates,
        hidden, place, turned,
    )
    near = shift(near, "c")
    far, far_other, near, other_down = lax.optimization_barrier((f0, h0, near, other_down))
    far, far_other = ring_gy(far, 1), ring_gy(far_other, -1, True)
    got = [payloads[0]] + [around(payloads[k], k) for k in (1, 2, 3)]
    block = pair_ordered(pair_ordered(got[0], got[1], c), pair_ordered(got[2], got[3], c), y)
    block = block.reshape(16, KQ + 2048)
    along = jnp.where(c == 0, z, x)

    def with_tail(k):
        own = lax.dynamic_slice_in_dim(block, KQ + (along + k) % 4 * 512, 512, 1)
        return jnp.concatenate([block[:, :KQ], own], axis=1)

    blocks = [with_tail(0)] + [crossed(with_tail(k), 0, k) for k in (1, 2, 3)]
    blocks, ffn_gain, ready = lax.optimization_barrier(
        (spread(place, blocks), ffn_gain, (down_weight, other_down, turned))
    )
    lower_weights = load(*ready[:2], "load_lower")
    own = own_quarter(place, ready[2])
    ffn_gain = ffn_gain.reshape(1, D)
    gains = chunked(ffn_gain)
    blocks = [blocks[0]] + [crossed(blocks[k], 1, k) for k in (1, 2, 3)]
    blocks, gains, lower_weights, own = lax.optimization_barrier(
        (blocks, gains, lower_weights, own)
    )
    kept, *sent, tail = project(
        place, blocks, own, near, (far, far_other)
    )
    taken = [around(sent[k - 1], k) for k in (1, 2, 3)]
    dispatched = mix(place, kept, taken, gains, tail)
    arrived = lax.all_to_all(dispatched, ("g", "z", "x", "y"), 0, 0, tiled=True)
    other = shift(arrived, "c")
    seen, squares, kept, sent, upper_weights = receive(
        place, arrived, gains, gate_weight.T, up_weight.T
    )
    taken = shift(sent, "c")
    sent, own = expert(place, seen, other, squares, gains, upper_weights)
    summed = lower(place, own, shift(sent, "c"), lower_weights, kept, taken, ffn_gain)
    returned = lax.all_to_all(summed, ("g", "z", "x", "y"), 0, 0, tiled=True)
    return combine(returned, parts)


def solution(mesh):
    fine = Mesh(mesh.devices.reshape(*SIZES.values()), ALL)
    rows = P(ALL, None)
    return jax.shard_map(
        per_device,
        mesh=fine,
        in_specs=(
            rows,
            rows,
            rows,
            rows,
            P(ALL, None, None),
            P(ALL, None, None),
            P(ALL),
            P(None, SECTION),
            P(),
            P(None, ALL),
            P(None, ALL),
            rows,
            rows,
            rows,
        ),
        out_specs=rows,
        check_vma=False,
    )
```

```python
import math

import jax
import jax.numpy as jnp
from jax import lax
from jax.experimental import pallas as pl
from jax.experimental.pallas import tpu as pltpu
from jax.sharding import Mesh, PartitionSpec as P

D = 7168
HEAD = 256
KALL = 16384
KHALF = KALL // 2
KQ = KHALF // 2
HID_DEV = 320
COLS = 112
EXPERTS = 8
BF = jnp.bfloat16
F32 = jnp.float32
SIZES = {"g": 2, "z": 4, "x": 4, "y": 2, "c": 2}
ALL = ("g", "z", "x", "y", "c")
SECTION = ("z", "x", "y", "c")


def shift(array, axis, step=1):
    n = SIZES[axis]
    return lax.ppermute(array, axis, [(i, (i + step) % n) for i in range(n)])


def others4(array, axis):
    return [shift(array, axis, 1), shift(array, axis, 2), shift(array, axis, 3)]


def ring_gy(array, step, swap=False):
    pairs = [
        (i * 2 + core, (i + step) % 4 * 2 + (1 - core if swap else core))
        for i in range(4)
        for core in range(2)
    ]
    return lax.ppermute(array, ("g", "y", "c"), pairs)


def around(array, k):
    return lax.ppermute(array, ("y", "c"), [(i, i ^ k) for i in range(4)])


def crossed(array, stage, step):
    pairs = []
    for z in range(4):
        for x in range(4):
            for c in range(2):
                along_z = c == stage
                to = ((z + step) % 4, x) if along_z else (z, (x + step) % 4)
                pairs.append(((z * 4 + x) * 2 + c, (to[0] * 4 + to[1]) * 2 + c))
    return lax.ppermute(array, ("z", "x", "c"), pairs)


def pair_ordered(own, other, mine):
    return jnp.where(
        mine == 0, jnp.stack([own, other]), jnp.stack([other, own])
    )


VMEM = pl.BlockSpec(memory_space=pltpu.VMEM)
SMEM = pl.BlockSpec(memory_space=pltpu.SMEM)
HBM = pl.BlockSpec(memory_space=pltpu.HBM)


def in_hbm(array):
    return pltpu.with_memory_space_constraint(array, pltpu.HBM)


def row_of(value, row):
    here = lax.broadcasted_iota(jnp.int32, value.shape, 0) == row
    return jnp.sum(jnp.where(here, value, 0.0), axis=0, keepdims=True)


def attend_kernel(
    lengths, routes, route_gates, place, q, hidden, k, v, new_key, new_value, turned,
    p0, p1, p2, p3, f0, h0, near, parts,
    keys, values, heads_of, flat, tails, sems,
):
    rows = q.shape[0]
    y, c = place[2], place[3]
    cuts = []
    for n, (of_c, of_y, part) in enumerate(((c, 1 - y, f0), (1 - c, 1 - y, h0), (1 - c, y, near))):
        at = pl.multiple_of(of_c * KHALF + of_y * KQ, KQ)
        cuts.append(pltpu.make_async_copy(
            turned.at[:, pl.ds(at, KQ)], part, sems.at[3, n]
        ))
    copies = [
        [
            pltpu.make_async_copy(source.at[r], kept.at[r], sems.at[i, r])
            for i, (source, kept) in enumerate(((k, keys), (v, values)))
        ]
        for r in range(rows)
    ]
    for copy in [copies[r][i] for p in range(0, rows, 2) for i in range(2) for r in (p, p + 1)]:
        copy.start()
    for copy in cuts:
        copy.start()
    scaling = 1.0 / math.sqrt(HEAD)
    scaled = q[...].astype(F32) * scaling
    for h in range(heads_of.shape[1]):
        heads_of[:, h, :] = scaled[:, h * HEAD : (h + 1) * HEAD]

    lane = lax.broadcasted_iota(jnp.int32, (1, 128), 1) - COLS
    line = lax.broadcasted_iota(jnp.int32, (rows, 128), 0)
    count = jnp.zeros((1, 128), F32)
    slots = jnp.zeros((rows, 128), F32)
    for r in range(rows):
        named = (lane == routes[r, 0]) | (lane == routes[r, 1]) | (lane == routes[r, 2])
        count = count + jnp.where(named, 1.0, 0.0)
        slots = slots + jnp.where((line == r) & named, count, 0.0)
    spot = lax.broadcasted_iota(jnp.int32, (1, 128), 1)
    half = lax.broadcasted_iota(jnp.int32, (2 * rows, 128), 0)
    of_expert, of_slot = spot // 16, spot % 2
    used = jnp.zeros((1, 128), jnp.int32)
    combined = jnp.zeros((2 * rows, 128), F32)
    for r in range(rows):
        gates = [jnp.full((1, 128), route_gates[r, k], jnp.int32).astype(F32) for k in range(3)]
        named = [of_expert == routes[r, k] for k in range(3)]
        chosen = jnp.zeros((1, 128), F32)
        for k in range(3):
            chosen = chosen + jnp.where(named[k], gates[k], 0.0)
        share = chosen / (gates[0] + gates[1] + gates[2])
        here = named[0] | named[1] | named[2]
        share = jnp.where(here & (used == of_slot), share, 0.0)
        used = used + jnp.where(here, 1, 0)
        high = share.astype(BF).astype(F32)
        combined = combined + jnp.where(half == r, high, 0.0)
        combined = combined + jnp.where(half == rows + r, share - high, 0.0)
    parts[...] = combined.astype(BF)
    stream = hidden[...].astype(F32)
    blank = jnp.zeros((rows, 128 - COLS), F32)
    for z in range(4):
        for x in range(4):
            for iy in range(2):
                for ic in range(2):
                    chunk = ((z * 4 + x) * 2 + iy) * 2 + ic
                    at = (x * 4 + z if ic else z * 4 + x) * 128
                    part = stream[:, chunk * COLS : (chunk + 1) * COLS]
                    part = jnp.concatenate([part, blank], axis=1) + slots
                    tails[ic * 2 + iy, :, at : at + 128] = part.astype(BF)

    own_keys, own_values = new_key[...].astype(F32), new_value[...].astype(F32)
    for pair in range(0, rows, 2):
        probs, own_probs = [], []
        for r in (pair, pair + 1):
            copies[r][0].wait()
        for r in (pair, pair + 1):
            queried = heads_of[r]
            itself = jnp.sum(queried * row_of(own_keys, r), axis=1, keepdims=True)
            cached = lax.dot_general(
                queried.astype(BF), keys[r], (((1,), (1,)), ((), ())),
                preferred_element_type=F32,
            )
            position = lax.broadcasted_iota(jnp.int32, cached.shape, 1)
            cached = jnp.where(position < lengths[r], cached, -jnp.inf)
            highest = jnp.maximum(jnp.max(cached, axis=1, keepdims=True), itself)
            cached_exp = jnp.exp(cached - highest)
            itself_exp = jnp.exp(itself - highest)
            share = 1.0 / (jnp.sum(cached_exp, axis=1, keepdims=True) + itself_exp)
            probs.append((cached_exp * share).astype(BF))
            own_probs.append((itself_exp * share).astype(BF).astype(F32))
        for r in (pair, pair + 1):
            copies[r][1].wait()
        for i, r in enumerate((pair, pair + 1)):
            mixture = jnp.dot(probs[i], values[r], preferred_element_type=F32)
            mixture = mixture + own_probs[i] * row_of(own_values, r)
            for h in range(mixture.shape[0]):
                at = h % 16 * HEAD
                flat[h // 16, r : r + 1, at : at + HEAD] = mixture[h : h + 1, :]
    for k, out in enumerate((p0, p1, p2, p3)):
        of_c = 1 - c if k % 2 else c
        of_y = 1 - y if k // 2 else y
        out[:, :KQ] = flat[of_c * 2 + of_y].astype(BF)
        out[:, KQ:] = tails[of_c * 2 + of_y]
    for copy in cuts:
        copy.wait()


def attend(
    queries, new_key, new_value, cache_keys, cache_values, lengths, routes, route_gates, hidden,
    place, turned,
):
    rows, context = cache_keys.shape[0], cache_keys.shape[1]
    heads = queries.shape[1] // HEAD
    return pl.pallas_call(
        attend_kernel,
        out_shape=(
            *(jax.ShapeDtypeStruct((rows, KQ + 16 * 128), BF),) * 4,
            jax.ShapeDtypeStruct((COLS, KQ), BF),
            jax.ShapeDtypeStruct((COLS, KQ), BF),
            jax.ShapeDtypeStruct((COLS, KQ), BF),
            jax.ShapeDtypeStruct((2 * rows, 128), BF),
        ),
        in_specs=[SMEM] * 4 + [VMEM] * 2 + [HBM] * 2 + [VMEM] * 2 + [HBM],
        out_specs=(VMEM,) * 8,
        scratch_shapes=[
            pltpu.VMEM((rows, context, HEAD), BF),
            pltpu.VMEM((rows, context, HEAD), BF),
            pltpu.VMEM((rows, heads, HEAD), F32),
            pltpu.VMEM((4, rows, KQ), F32),
            pltpu.VMEM((4, rows, 16 * 128), BF),
            pltpu.SemaphoreType.DMA((4, rows)),
        ],
        compiler_params=pltpu.CompilerParams(vmem_limit_bytes=24 << 20),
        cost_estimate=pl.CostEstimate(
            flops=4 * rows * heads * context * HEAD,
            bytes_accessed=4 * rows * context * HEAD,
            transcendentals=rows * heads * context,
        ),
        name="attend",
    )(
        in_hbm(lengths),
        in_hbm(routes),
        in_hbm(route_gates),
        place,
        in_hbm(queries),
        in_hbm(hidden),
        in_hbm(cache_keys),
        in_hbm(cache_values),
        in_hbm(new_key),
        in_hbm(new_value),
        in_hbm(turned),
    )


def at16(index):
    return pl.multiple_of(index, 16)


def spread_kernel(place, b0, b1, b2, b3, o0, o1, o2, o3):
    z, x, c = place[0], place[1], place[3]
    second = jnp.where(c == 0, x, z)
    for i, block in enumerate((b0, b1, b2, b3)):
        rows = slice(16 * i, 16 * i + 16)
        for k, out in enumerate((o0, o1, o2, o3)):
            out[rows, :KQ] = block[:, :KQ]
            lanes = pl.multiple_of(KQ + (second + k) % 4 * 128, 128)
            out[rows, KQ:] = block[:, pl.ds(lanes, 128)]


def spread(place, blocks):
    return pl.pallas_call(
        spread_kernel,
        out_shape=(jax.ShapeDtypeStruct((64, KQ + 128), BF),) * 4,
        in_specs=[SMEM] + [VMEM] * 4,
        out_specs=(VMEM,) * 4,
        compiler_params=pltpu.CompilerParams(vmem_limit_bytes=8 << 20),
        name="spread",
    )(place, *blocks)


def own_kernel(place, turned, out, sem):
    y, c = place[2], place[3]
    quarter = pl.ds(pl.multiple_of(c * KHALF + y * KQ, KQ), KQ)
    copy = pltpu.make_async_copy(turned.at[:, quarter], out, sem.at[0])
    copy.start()
    copy.wait()


def own_quarter(place, turned):
    return pl.pallas_call(
        own_kernel,
        out_shape=jax.ShapeDtypeStruct((COLS, KQ), BF),
        in_specs=[SMEM, HBM],
        out_specs=VMEM,
        scratch_shapes=[pltpu.SemaphoreType.DMA((1,))],
        compiler_params=pltpu.CompilerParams(vmem_limit_bytes=4 << 20),
        name="own_quarter",
    )(place, in_hbm(turned))


def project_kernel(
    place, r0, r1, r2, r3, own, other, far, far_other, kept, s1, s2, s3, tail, rows
):
    z, x, c = place[0], place[1], place[3]
    for k, block in enumerate((r0, r1, r2, r3)):
        for i in range(4):
            of_z = (z - jnp.where(c == 0, i, k) + 4) % 4
            of_x = (x - jnp.where(c == 0, k, i) + 4) % 4
            row = at16(of_z * 64 + of_x * 16)
            rows[pl.ds(row, 16), :] = block[16 * i : 16 * i + 16, :KQ]
            tail[pl.ds(row, 16), :] = block[16 * i : 16 * i + 16, KQ:]
    weights = jnp.concatenate([own[...], other[...], far[...], far_other[...]], axis=0)
    product = lax.dot_general(
        weights, rows[...], (((1,), (1,)), ((), ())), preferred_element_type=F32
    )
    kept[...] = product[:COLS]
    for i, sent in enumerate((s1, s2, s3)):
        sent[...] = product[(i + 1) * COLS : (i + 2) * COLS].astype(BF)


def project(place, blocks, own, other, fars):
    return pl.pallas_call(
        project_kernel,
        out_shape=(
            jax.ShapeDtypeStruct((COLS, 256), F32),
            *(jax.ShapeDtypeStruct((COLS, 256), BF),) * 3,
            jax.ShapeDtypeStruct((256, 128), BF),
        ),
        in_specs=[SMEM] + [VMEM] * 8,
        out_specs=(VMEM,) * 5,
        scratch_shapes=[
            pltpu.VMEM((256, KQ), BF),
        ],
        compiler_params=pltpu.CompilerParams(vmem_limit_bytes=12 << 20),
        name="project",
    )(place, *blocks, own, other, *fars)


def chunk_kernel(gain, out):
    for i in range(D // COLS):
        out[i : i + 1, :] = gain[:, i * COLS : (i + 1) * COLS]


def chunked(gain):
    return pl.pallas_call(
        chunk_kernel,
        out_shape=jax.ShapeDtypeStruct((D // COLS, COLS), F32),
        in_specs=[VMEM],
        out_specs=VMEM,
        compiler_params=pltpu.CompilerParams(vmem_limit_bytes=2 << 20),
        name="chunked",
    )(gain)


def mix_kernel(place, kept, r1, r2, r3, gains, tail, dispatched):
    chunk = ((place[0] * 4 + place[1]) * 2 + place[2]) * 2 + place[3]
    projected = kept[...] + r1[...].astype(F32) + (r2[...].astype(F32) + r3[...].astype(F32))
    back = tail[...].astype(F32).T[:COLS]
    widened = (back + projected).astype(BF).astype(F32)
    column = jnp.broadcast_to(row_of(gains[...], chunk), (8, COLS)).T[:, :1]
    carried = (widened * column).astype(BF)
    position = lax.broadcasted_iota(jnp.int32, (256, 128), 0)
    slot = lax.broadcasted_iota(jnp.int32, (256, 128), 1)
    z, x, y, c = position // 64, position // 16 % 4, position // 8 % 2, position // 4 % 2
    here = ((c * 4 + z) * 4 + x) * 2 + y == slot // 2
    rank = (slot % 2 + 1).astype(F32)
    ranks = tail[...].astype(F32)
    for e in range(EXPERTS):
        pick = jnp.where(here & (ranks[:, COLS + e : COLS + e + 1] == rank), 1.0, 0.0).astype(BF)
        block = jnp.dot(carried, pick, preferred_element_type=F32).astype(BF)
        for device in range(8):
            dispatched[8 * e + device] = block


def mix(place, kept, taken, gains, tail):
    return pl.pallas_call(
        mix_kernel,
        out_shape=jax.ShapeDtypeStruct((64, COLS, 128), BF),
        in_specs=[SMEM] + [VMEM] * 6,
        out_specs=VMEM,
        compiler_params=pltpu.CompilerParams(vmem_limit_bytes=12 << 20),
        name="mix",
    )(place, kept, *taken, gains, tail)


def load_kernel(first, second, out, sems):
    copies = []
    for i, source in enumerate((first, second)):
        for k in range(4):
            lanes = pl.ds(k * (D // 4), D // 4)
            copies.append(pltpu.make_async_copy(
                source.at[:, lanes], out.at[pl.ds(i * HID_DEV, HID_DEV), lanes], sems.at[i, k]
            ))
    for copy in copies:
        copy.start()
    for copy in copies:
        copy.wait()


def load(first, second, name):
    return pl.pallas_call(
        load_kernel,
        out_shape=jax.ShapeDtypeStruct((2 * HID_DEV, D), BF),
        in_specs=[HBM] * 2,
        out_specs=VMEM,
        scratch_shapes=[pltpu.SemaphoreType.DMA((2, 4))],
        compiler_params=pltpu.CompilerParams(vmem_limit_bytes=16 << 20),
        cost_estimate=pl.CostEstimate(
            flops=0, bytes_accessed=8 * HID_DEV * D, transcendentals=0
        ),
        name=name,
    )(in_hbm(first), in_hbm(second))


def squares_of(block, scales, chunk_of_c):
    i, c = chunk_of_c
    scale = jnp.where(c == 0, scales[:, 2 * i : 2 * i + 1], scales[:, 2 * i + 1 : 2 * i + 2])
    value = block.astype(F32) * scale
    return jnp.sum((value * value).reshape(14, 8, 128), axis=0)


def receive_kernel(
    place, arrived, gains, gate, up, columns, squares, kept, sent, weights, sems
):
    x, y, c = place[1], place[2], place[3]
    copies = []
    for i, source in enumerate((gate, up)):
        for k in range(4):
            lanes = pl.ds(k * (D // 4), D // 4)
            copies.append(pltpu.make_async_copy(
                source.at[:, lanes], weights.at[pl.ds(i * HID_DEV, HID_DEV), lanes], sems.at[i, k]
            ))
    for copy in copies:
        copy.start()
    scales = 1.0 / gains[...].T
    for g in range(2):
        total = jnp.zeros((8, 128), F32)
        lanes = slice(128 * g, 128 * g + 128)
        for i in range(32):
            block = arrived[32 * g + i]
            columns[pl.ds(at16((2 * i + c) * COLS), COLS), lanes] = block
            columns[pl.ds(at16((2 * i + 1 - c) * COLS), COLS), lanes] = jnp.zeros_like(block)
            total = total + squares_of(block, scales, (i, c))
        squares[:, lanes] = total
    row = lax.broadcasted_iota(jnp.int32, (32, 256), 0)
    lane = lax.broadcasted_iota(jnp.int32, (32, 256), 1)
    of_c = jnp.where(row < 16, c, 1 - c)
    slot = ((of_c * 4 + row // 2 % 4) * 4 + x) * 2 + y
    mine = lane == row // 8 % 2 * 128 + slot * 2 + row % 2
    residual = lax.dot_general(
        jnp.where(mine, 1.0, 0.0).astype(BF), columns[...],
        (((1,), (1,)), ((), ())), preferred_element_type=F32,
    ).astype(BF)
    kept[...] = residual[:16]
    sent[...] = residual[16:]
    for copy in copies:
        copy.wait()


def receive(place, arrived, gains, gate, up):
    return pl.pallas_call(
        receive_kernel,
        out_shape=(
            jax.ShapeDtypeStruct((D, 256), BF),
            jax.ShapeDtypeStruct((8, 256), F32),
            jax.ShapeDtypeStruct((16, D), BF),
            jax.ShapeDtypeStruct((16, D), BF),
            jax.ShapeDtypeStruct((2 * HID_DEV, D), BF),
        ),
        in_specs=[SMEM] + [VMEM] * 2 + [HBM] * 2,
        out_specs=(VMEM,) * 5,
        scratch_shapes=[pltpu.SemaphoreType.DMA((2, 4))],
        compiler_params=pltpu.CompilerParams(vmem_limit_bytes=16 << 20),
        name="receive",
    )(place, arrived, gains, in_hbm(gate), in_hbm(up))


def expert_kernel(place, seen, other, own_squares, gains, weights, sent, kept, columns, act):
    c = place[3]
    scales = 1.0 / gains[...].T
    other_squares = [jnp.zeros((8, 128), F32)] * 2
    for i in range(32):
        own_rows = pl.ds(at16((2 * i + c) * COLS), COLS)
        other_rows = pl.ds(at16((2 * i + 1 - c) * COLS), COLS)
        columns[own_rows, :] = seen[own_rows, :]
        for g in range(2):
            block = other[32 * g + i]
            columns[other_rows, 128 * g : 128 * g + 128] = block
            other_squares[g] = other_squares[g] + squares_of(block, scales, (i, 1 - c))
    product = jnp.dot(weights[...], columns[...], preferred_element_type=F32)
    squares = own_squares[...] + jnp.concatenate(other_squares, axis=1)
    scale = lax.rsqrt(jnp.sum(squares, axis=0, keepdims=True) / D + 1e-05)
    gated = product[:HID_DEV] * scale
    upward = product[HID_DEV:] * scale
    activated = gated / (1.0 + jnp.exp(-gated)) * upward
    act[...] = activated.T.astype(BF)
    for g in range(2):
        sent[g * 64 : g * 64 + 64, :] = act[pl.ds(at16(g * 128 + (1 - c) * 64), 64), :]
        kept[g * 64 : g * 64 + 64, :] = act[pl.ds(at16(g * 128 + c * 64), 64), :]


def expert(place, seen, other, own_squares, gains, weights):
    return pl.pallas_call(
        expert_kernel,
        out_shape=(jax.ShapeDtypeStruct((128, HID_DEV), BF),) * 2,
        in_specs=[SMEM] + [VMEM] * 5,
        out_specs=(VMEM,) * 2,
        scratch_shapes=[pltpu.VMEM((D, 256), BF), pltpu.VMEM((256, HID_DEV), BF)],
        compiler_params=pltpu.CompilerParams(vmem_limit_bytes=16 << 20),
        name="expert",
    )(place, seen, other, own_squares, gains, weights)


def lower_kernel(place, own, other, weights, kept, taken, gain, out, act):
    x, y = place[1], place[2]
    act[:, :HID_DEV] = own[...]
    act[:, HID_DEV : 2 * HID_DEV] = other[...]
    row = lax.broadcasted_iota(jnp.int32, (128, 32), 0)
    column = lax.broadcasted_iota(jnp.int32, (128, 32), 1) % 16
    here = (row // 2 % 8 == x * 2 + y) & (row // 16 * 2 + row % 2 == column)
    act[:, 2 * HID_DEV :] = jnp.where(here, 1.0, 0.0).astype(BF)
    width = D // 4
    for k in range(4):
        lanes = slice(k * width, (k + 1) * width)
        residual = (kept[:, lanes] + taken[:, lanes]).astype(F32) / gain[:, lanes]
        high = residual.astype(BF)
        low = (residual - high.astype(F32)).astype(BF)
        depth = jnp.concatenate([weights[:, lanes], high, low], axis=0)
        part = jnp.dot(act[...], depth, preferred_element_type=F32)
        out[:, :, lanes] = part.astype(BF).reshape(64, 2, width)


def lower(place, own, other, weights, kept, taken, gain):
    return pl.pallas_call(
        lower_kernel,
        out_shape=jax.ShapeDtypeStruct((64, 2, D), BF),
        in_specs=[SMEM] + [VMEM] * 6,
        out_specs=VMEM,
        scratch_shapes=[pltpu.VMEM((128, 2 * HID_DEV + 32), BF)],
        compiler_params=pltpu.CompilerParams(vmem_limit_bytes=16 << 20),
        name="lower",
    )(place, own, other, weights, kept, taken, gain)


def combine_kernel(returned, weights, out):
    rows = out.shape[0]
    width = D // 4
    for k in range(4):
        lanes = slice(k * width, (k + 1) * width)
        sums = returned[:, :, lanes].reshape(128, width)
        total = jnp.dot(weights[...], sums, preferred_element_type=F32)
        out[:, lanes] = (total[:rows] + total[rows:]).astype(BF)


def combine(returned, weights):
    return pl.pallas_call(
        combine_kernel,
        out_shape=jax.ShapeDtypeStruct((weights.shape[0] // 2, D), BF),
        in_specs=[VMEM] * 2,
        out_specs=VMEM,
        compiler_params=pltpu.CompilerParams(vmem_limit_bytes=8 << 20),
        name="combine",
    )(returned, weights)


def per_device(
    hidden,
    queries,
    new_key,
    new_value,
    cache_keys,
    cache_values,
    lengths,
    out_weight,
    ffn_gain,
    gate_weight,
    up_weight,
    down_weight,
    routes,
    route_gates,
):
    z, x, y, c = (lax.axis_index(a) for a in SECTION)
    chunk = ((z * 4 + x) * 2 + y) * 2 + c
    place = jnp.stack([z, x, y, c]).astype(jnp.int32)

    turned = out_weight.T

    other_down = shift(down_weight, "c")
    *payloads, f0, h0, near, parts = attend(
        queries, new_key, new_value, cache_keys, cache_values, lengths, routes, route_gates,
        hidden, place, turned,
    )
    near = shift(near, "c")
    far, far_other, near, other_down = lax.optimization_barrier((f0, h0, near, other_down))
    far, far_other = ring_gy(far, 1), ring_gy(far_other, -1, True)
    got = [payloads[0]] + [around(payloads[k], k) for k in (1, 2, 3)]
    block = pair_ordered(pair_ordered(got[0], got[1], c), pair_ordered(got[2], got[3], c), y)
    block = block.reshape(16, KQ + 2048)
    along = jnp.where(c == 0, z, x)

    def with_tail(k):
        own = lax.dynamic_slice_in_dim(block, KQ + (along + k) % 4 * 512, 512, 1)
        return jnp.concatenate([block[:, :KQ], own], axis=1)

    blocks = [with_tail(0)] + [crossed(with_tail(k), 0, k) for k in (1, 2, 3)]
    blocks, ffn_gain, ready = lax.optimization_barrier(
        (spread(place, blocks), ffn_gain, (down_weight, other_down, turned))
    )
    lower_weights = load(*ready[:2], "load_lower")
    own = own_quarter(place, ready[2])
    ffn_gain = ffn_gain.reshape(1, D)
    gains = chunked(ffn_gain)
    blocks = [blocks[0]] + [crossed(blocks[k], 1, k) for k in (1, 2, 3)]
    blocks, gains, lower_weights, own = lax.optimization_barrier(
        (blocks, gains, lower_weights, own)
    )
    kept, *sent, tail = project(
        place, blocks, own, near, (far, far_other)
    )
    taken = [around(sent[k - 1], k) for k in (1, 2, 3)]
    dispatched = mix(place, kept, taken, gains, tail)
    arrived = lax.all_to_all(dispatched, ("g", "z", "x", "y"), 0, 0, tiled=True)
    other = shift(arrived, "c")
    seen, squares, kept, sent, upper_weights = receive(
        place, arrived, gains, gate_weight.T, up_weight.T
    )
    taken = shift(sent, "c")
    sent, own = expert(place, seen, other, squares, gains, upper_weights)
    summed = lower(place, own, shift(sent, "c"), lower_weights, kept, taken, ffn_gain)
    returned = lax.all_to_all(summed, ("g", "z", "x", "y"), 0, 0, tiled=True)
    return combine(returned, parts)


def solution(mesh):
    fine = Mesh(mesh.devices.reshape(*SIZES.values()), ALL)
    rows = P(ALL, None)
    return jax.shard_map(
        per_device,
        mesh=fine,
        in_specs=(
            rows,
            rows,
            rows,
            rows,
            P(ALL, None, None),
            P(ALL, None, None),
            P(ALL),
            P(None, SECTION),
            P(),
            P(None, ALL),
            P(None, ALL),
            rows,
            rows,
            rows,
        ),
        out_specs=rows,
        check_vma=False,
    )
```
